32 devices in a mesh: fsdp: 4 (over y, x), dp: 8 (over z, core).
Axes of the slice: x: 2, y: 2, z: 4, core: 2. Of those that a mesh axis runs over, the one named last changes fastest.
Arguments:
- tokens: bfloat16 [4096, 4096], P(('fsdp', 'dp')), may hold values from -6 to 6
- master_old: float32 [480, 128, 128], P(('fsdp', 'dp')), may hold values from -0.25 to 0.25
- moment_old: float32 [480, 128, 128], P(('fsdp', 'dp')), may hold values from -6 to 6
- second_old: float32 [480, 128, 128], P(('fsdp', 'dp')), may hold values from 0.01 to 1
- old_cell: int32 [112, 4], P('fsdp'), may hold values from 0 to 119, as said below
- new_cell: int32 [112, 4], P('fsdp'), may hold values from 0 to 119, as said below
- regrown: int32 [112, 4], P('fsdp'), may hold values 0 or 1
- new_rows: int32 [112, 4], replicated, may hold values from 0 to 31, as said below
Outputs:
- hidden: bfloat16 [4096, 14336], P(('fsdp', 'dp'))
- master_new: float32 [480, 128, 128], P(('fsdp', 'dp'))
- moment_new: float32 [480, 128, 128], P(('fsdp', 'dp'))
- second_new: float32 [480, 128, 128], P(('fsdp', 'dp'))
The draws below stay inside these ranges and needn't reach their ends.
Inputs may be any that keep to these rules, and one draw needn't show every extreme that they name: `old_cell`: within one fsdp index, taking its slots column by column and then by k, the old cells strictly increase; a cell's index // 15 is its holder along dp and index % 15 its place in that holder's buffer. `new_cell`: strictly increasing in the same order; every slot's new cell differs from its old cell by at most 8, and by exactly 8 for some slot of every fsdp index. `new_rows`: the 4 block rows of one block column are distinct.
All inputs are finite; a program needn't handle non-finite values. No bound on the sum of `regrown` on one device may be relied on, other than what follows from the above.
Results may differ from the reference program's by a relative error of at most 0.007.
Values may be sent and summed in bfloat16 or wider, within the bound.
A program may use at most 128 MiB of HBM per device.

```python
import math
import jax
import jax.numpy as jnp
from jax import lax

D = 4096
FF = 14336
BLK = 128
NZC = 4
NBR = 32
NBC = 112
BCF = 28
SLOTS = 112
CELLS = 120
HOLES = 8
STORE = 480
TOKENS = 4096
N_FSDP = 4


def cell_pair(key):
    subkeys = jax.random.split(jax.random.fold_in(key, 11), 4)
    pivot = jax.random.randint(subkeys[0], (N_FSDP, 1, 1), 0, SLOTS)
    raw_old = jax.random.randint(subkeys[1], (N_FSDP, HOLES, 1), 0, 1 << 20)
    raw_new = jax.random.randint(subkeys[2], (N_FSDP, HOLES, 1), 0, 1 << 20)
    cuts_old = pivot + 1 + raw_old % (SLOTS - pivot)
    cuts_new = raw_new % (pivot + 1)
    index = jnp.arange(SLOTS, dtype=jnp.int32)[None, None, :]
    shift_old = jnp.sum((cuts_old <= index).astype(jnp.int32), axis=1)
    shift_new = jnp.sum((cuts_new <= index).astype(jnp.int32), axis=1)
    base = jnp.arange(SLOTS, dtype=jnp.int32)[None, :]
    old_cells = (base + shift_old).astype(jnp.int32)
    new_cells = (base + shift_new).astype(jnp.int32)
    ranking = jax.random.permutation(subkeys[3], N_FSDP)
    mirrored = (ranking < N_FSDP // 2)[:, None]
    old_cells = jnp.where(mirrored, CELLS - 1 - old_cells[:, ::-1], old_cells)
    new_cells = jnp.where(mirrored, CELLS - 1 - new_cells[:, ::-1], new_cells)
    return (old_cells.reshape(NBC, NZC).astype(jnp.int32), new_cells.reshape(NBC, NZC).astype(jnp.int32))


def draw_old_cell(key, part):
    return cell_pair(key)[0]


def draw_new_cell(key, part):
    return cell_pair(key)[1]


def draw_new_rows(key, part):
    subkeys = jax.random.split(jax.random.fold_in(key, 23), NBC)
    picks = jax.vmap(lambda sub: jax.random.permutation(sub, NBR)[:NZC])(subkeys)
    return picks.astype(jnp.int32)


def touch_ends(drawn, own_key, smallest, top_value):
    longest = drawn.shape.index(max(drawn.shape))
    spots = []
    for shift in (0, 1):
        where = [jax.random.randint(jax.random.fold_in(own_key, axis), (), 0, length) for axis, length in enumerate(drawn.shape)]
        where[longest] = (where[longest] + shift) % drawn.shape[longest]
        spots.append(tuple(where))
    return drawn.at[spots[0]].set(smallest).at[spots[1]].set(top_value)


def levels(key, shape, shards, least, top_value):
    factor_of = 1.0
    for dim, shards_of in shards:
        heights = jax.random.uniform(jax.random.fold_in(jax.random.fold_in(key, 6), dim), (shards_of,), jnp.float32, least / len(shards), top_value / len(shards))
        factor_of = factor_of * jnp.repeat(jnp.exp(heights), shape[dim] // shards_of).reshape((-1,) + (1,) * (len(shape) - 1 - dim))
    return factor_of


def noise(stream_key, dims, deviation, limit, cuts=(), held_as=jnp.bfloat16):
    array = deviation * jax.random.normal(stream_key, dims, jnp.float32)
    if cuts:
        array = array * levels(stream_key, dims, cuts, -0.22, 0.18)
    return jnp.clip(array, -limit, limit).astype(held_as)


def setup_inputs(seed: int = 0) -> dict:
    key_list = jax.random.split(jax.random.key(seed), 9)
    return {
        "tokens": noise(key_list[0], (TOKENS, D), 1.0, 6.0, ((0, 32),)),
        "master_old": noise(key_list[1], (STORE, BLK, BLK), (NZC * BLK) ** -0.5, 0.25, ((0, 32),), jnp.float32),
        "moment_old": noise(key_list[2], (STORE, BLK, BLK), 1.0, 6.0, ((0, 32),), jnp.float32),
        "second_old": jnp.clip(jnp.exp(math.log(1.0) - 4.6051702 * jax.random.uniform(key_list[3], (STORE, BLK, BLK), jnp.float32) ** levels(key_list[3], (STORE, BLK, BLK), ((0, 32),), -0.2, 0.2)), 0.01, 1.0),
        "old_cell": draw_old_cell(jax.random.fold_in(key_list[8], 71), 0),
        "new_cell": draw_new_cell(jax.random.fold_in(key_list[8], 71), 0),
        "regrown": touch_ends((jax.random.randint(key_list[6], (NBC, NZC), 0, 10) < 3).astype(jnp.int32), jax.random.fold_in(key_list[6], 1), 0, 1),
        "new_rows": draw_new_rows(jax.random.fold_in(key_list[8], 71), 0),
    }


def reference(tokens, master_old, moment_old, second_old, old_cell, new_cell, regrown, new_rows):
    groups = (jnp.arange(NBC, dtype=jnp.int32) // BCF).astype(jnp.int32)
    old_place = (groups[:, None] * CELLS + old_cell).reshape(-1).astype(jnp.int32)
    new_place = (groups[:, None] * CELLS + new_cell).reshape(-1).astype(jnp.int32)
    keep_flag = (regrown.reshape(-1) == 0)

    def migrate(buffer):
        moved = jnp.where(keep_flag[:, None, None], buffer[old_place], jnp.zeros((), buffer.dtype))
        placed = jnp.zeros_like(buffer).at[new_place].set(moved)
        return moved, placed

    master_moved, master_new = migrate(master_old)
    moment_moved, moment_new = migrate(moment_old)
    second_moved, second_new = migrate(second_old)
    weight_block = master_moved.astype(jnp.bfloat16).reshape(NBC, NZC, BLK, BLK)
    token_blocks = tokens.reshape(TOKENS, NBR, BLK)

    def column(inputs):
        row_index, block_set = inputs
        picked = jnp.take(token_blocks, row_index.astype(jnp.int32), axis=1).reshape(TOKENS, NZC * BLK)
        product = jnp.dot(picked, block_set.reshape(NZC * BLK, BLK), preferred_element_type=jnp.float32)
        return product.astype(jnp.bfloat16)

    stacked = lax.map(column, (new_rows, weight_block))
    hidden = jnp.transpose(stacked, (1, 0, 2)).reshape(TOKENS, FF)
    return hidden, master_new, moment_new, second_new
```

```python
import functools

import jax
import jax.numpy as jnp
from jax import lax
from jax.experimental import pallas as pl
from jax.experimental.pallas import tpu as pltpu
from jax.sharding import PartitionSpec as P

MESH = pl.DeviceIdType.MESH
PIECES = 3
X, Y, UP, DOWN, TWIN = range(5)


def passed_along(block, axis, distance):
    devices = range(lax.axis_size(axis))
    route = [(i - distance, i) for i in devices if i - distance in devices]
    return lax.ppermute(block, axis, route)


def sources(old_cell, new_cell, regrown, capacity):
    old_flat, new_flat = old_cell.reshape(-1), new_cell.reshape(-1)
    kept = jnp.where(regrown.reshape(-1) == 0, old_flat, -1)
    my_cells = lax.axis_index("dp") * capacity + jnp.arange(capacity, dtype=jnp.int32)
    matches = new_flat[None, :] == my_cells[:, None]
    return jnp.max(jnp.where(matches, kept[None, :], -1), axis=1)


def on_device_plain(tokens, master_old, moment_old, second_old, old_cell, new_cell, regrown, new_rows):
    capacity, block_size = master_old.shape[0], master_old.shape[1]
    column_count, nonzero_count = old_cell.shape
    width = lax.axis_size("dp")
    holes = width * capacity - column_count * nonzero_count
    farthest = min((holes + capacity - 1) // capacity, width - 1)
    holder = lax.axis_index("dp")
    source = sources(old_cell, new_cell, regrown, capacity)
    present = source >= 0
    source = jnp.maximum(source, 0)
    offset = holder - source // capacity
    candidate = jnp.where(offset > 0, 2 * offset - 1, jnp.where(offset < 0, -2 * offset, 0))
    pick_index = candidate * capacity + source % capacity
    shifts = [s for distance in range(1, farthest + 1) for s in (distance, -distance)]

    def settle(state):
        narrow = state.astype(jnp.bfloat16)
        pool = [state] + [passed_along(narrow, "dp", s).astype(jnp.float32) for s in shifts]
        chosen = jnp.take(jnp.concatenate(pool, axis=0), pick_index, axis=0, mode="clip")
        return jnp.where(present[:, None, None], chosen, jnp.float32(0.0))

    cells = lax.all_gather(master_old.astype(jnp.bfloat16), "dp", axis=0, tiled=True)
    panel = jnp.take(cells, old_cell.reshape(-1), axis=0)
    panel = jnp.where(regrown.reshape(-1)[:, None, None] == 0, panel, jnp.bfloat16(0))
    panel = panel.reshape(column_count, nonzero_count, block_size, block_size)
    panel = lax.all_gather(panel, "fsdp", axis=0, tiled=True)
    count, token_count = panel.shape[0], tokens.shape[0]
    token_blocks = tokens.reshape(token_count, tokens.shape[1] // block_size, block_size)
    picked = jnp.take(token_blocks, new_rows.reshape(-1), axis=1)
    picked = picked.reshape(token_count, count, nonzero_count, block_size)
    product = jnp.einsum("tcka,ckab->tcb", picked, panel, preferred_element_type=jnp.float32)
    hidden = product.reshape(token_count, count * block_size).astype(jnp.bfloat16)
    return hidden, settle(master_old), settle(moment_old), settle(second_old)


def arrival_order(levels):
    order = []
    for dz in range(1 - levels, levels):
        away = abs(dz)
        for piece in range(PIECES):
            if away:
                order.append((3 * (away - 1) + piece + 1, 0, dz, piece))
            for role in (1, 2):
                key = 1 + piece if not away else (5 + 2 * piece if away == 1 else 6 + 2 * away + piece)
                order.append((key + 0.1, role, dz, piece))
            if piece < 2:
                key = 5 if not away else 7 + 2 * away + piece
            else:
                key = 6 if not away else 7.5 + 2.5 * away
            order.append((key + 0.2, 3, dz, piece))
    return sorted(order)


def kernel(
    levels, holes, columns, nonzero,
    pack_ref, rows_ref, tokens_ref, master_ref, moment_ref, second_ref,
    hidden_ref, master_out, moment_out, second_out,
    own, side_x, side_y, corner, hid0, hid1, hid2, hid3,
    tok, tok_blocks, mas, mom, sec, mom_narrow, sec_narrow, mom_halo, sec_halo,
    new_mas, new_mom, new_sec, packs, plan,
    load_sem, store_sem, plan_sem, pack_send, pack_recv, halo_send, halo_recv, send_sem, recv_sem,
):
    f, h = lax.axis_index("fsdp"), lax.axis_index("dp")
    z, core = h // 2, lax.rem(h, 2)
    capacity, block = mas.shape[0], mas.shape[1]
    cells = 2 * levels * capacity
    cuts = [capacity * i // PIECES for i in range(PIECES + 1)]
    groups = (own, side_x, side_y, corner)
    hids = (hid0, hid1, hid2, hid3)

    loads = [
        pltpu.make_async_copy(src, dst, load_sem.at[i])
        for i, (src, dst) in enumerate(
            [(master_ref, mas), (moment_ref, mom), (second_ref, sec), (tokens_ref, tok)]
        )
    ]
    for copy in loads:
        copy.start()

    barrier = pltpu.get_barrier_semaphore()

    def at(role, level, which):
        return (jnp.bitwise_xor(f, role), level * 2 + which)

    def greet(device):
        pl.semaphore_signal(barrier, inc=1, device_id=device, device_id_type=MESH)

    up, down = z + 1 < levels, z > 0
    other = 1 - core
    crossing = jnp.where(core == 1, up, down)
    cross_level = jnp.where(core == 1, z + 1, z - 1)

    for group in groups:
        group[cells] = jnp.zeros((block, block), jnp.bfloat16)
    mom_halo[...] = jnp.zeros_like(mom_halo)
    sec_halo[...] = jnp.zeros_like(sec_halo)

    for role in (1, 2, 3):
        greet(at(role, z, core))
    greet(at(0, z, other))

    @pl.when(up)
    def _():
        greet(at(0, z + 1, core))

    @pl.when(down)
    def _():
        greet(at(0, z - 1, core))

    @pl.when(crossing)
    def _():
        greet(at(0, cross_level, other))

    loads[0].wait()
    for j in range(capacity):
        own[h * capacity + j] = mas[j].astype(jnp.bfloat16)
    pl.semaphore_wait(barrier, 4 + up.astype(jnp.int32) + down.astype(jnp.int32) + crossing.astype(jnp.int32))

    sent = []

    def piece_ref(role, level, which, piece):
        first = (level * 2 + which) * capacity + cuts[piece]
        return groups[role].at[pl.ds(first, cuts[piece + 1] - cuts[piece])]

    def when(condition, act):
        if condition is True:
            act()
        else:
            pl.when(condition)(act)

    def send(condition, way, role, level, piece):
        target = {
            X: lambda: at(1, z, core), Y: lambda: at(2, z, core),
            UP: lambda: at(0, z + 1, core), DOWN: lambda: at(0, z - 1, core),
            TWIN: lambda: at(0, z, other),
        }[way]()
        there = role ^ {X: 1, Y: 2}.get(way, 0)
        copy = pltpu.make_async_remote_copy(
            src_ref=piece_ref(role, level, core, piece),
            dst_ref=piece_ref(there, level, core, piece),
            send_sem=send_sem.at[way, role, piece, level],
            recv_sem=recv_sem.at[1 if way == TWIN else 0, there, piece, level],
            device_id=target,
            device_id_type=MESH,
        )
        when(condition, copy.start)
        sent.append((condition, copy))

    def await_piece(lane, role, level, which, piece):
        part = piece_ref(role, level, which, piece)
        pltpu.make_async_remote_copy(
            src_ref=part, dst_ref=part, send_sem=send_sem.at[0, 0, 0, 0],
            recv_sem=recv_sem.at[lane, role, piece, level],
            device_id=at(0, z, other), device_id_type=MESH,
        ).wait_recv()

    def both(a, b):
        if a is True:
            return b
        return jnp.logical_and(a, b)

    def handle(role, dz, piece):
        level = z + dz
        if dz == 0:
            here = True
        else:
            here = level < levels if dz > 0 else level >= 0
        if (role, dz) != (0, 0):
            when(here, lambda: await_piece(0, role, level, core, piece))
        even = lax.rem(level + 2 * levels, 2) == 0
        if role == 0 or (role == 3 and piece < 2):
            if dz >= 0:
                send(both(here, down), DOWN, role, level, piece)
            if dz <= 0:
                send(both(here, up), UP, role, level, piece)
        if role == 0:
            send(here, X, role, level, piece)
            send(here, Y, role, level, piece)
        if role == 2:
            if piece == 0 and dz == 0:
                send(here, X, role, level, piece)
            if piece == 2:
                send(both(here, even), X, role, level, piece)
        if role == 1:
            if piece == 1 and dz == 0:
                send(here, Y, role, level, piece)
            if piece == 2:
                send(both(here, jnp.logical_not(even)), Y, role, level, piece)
        send(here, TWIN, role, level, piece)

    def compute(role, first, last):
        group, hid = groups[role], hids[role]
        base = jnp.bitwise_xor(f, role) * columns

        def column(c, carry):
            left = [tok_blocks[rows_ref[base + c, k]] for k in range(nonzero)]
            right = [group[plan[role, 0, c * nonzero + k]] for k in range(nonzero)]
            total = jnp.dot(
                jnp.concatenate(left, axis=1), jnp.concatenate(right, axis=0),
                preferred_element_type=jnp.float32,
            )
            hid[:, pl.ds(pl.multiple_of(c * block, block), block)] = total.astype(jnp.bfloat16)
            return carry

        lax.fori_loop(first, last, column, 0)

    for piece in range(PIECES):
        handle(0, 0, piece)

    pack_copies = []
    for role in (1, 2, 3):
        copy = pltpu.make_async_remote_copy(
            src_ref=pack_ref, dst_ref=packs.at[role - 1],
            send_sem=pack_send.at[role - 1], recv_sem=pack_recv.at[role - 1],
            device_id=at(role, z, core), device_id_type=MESH,
        )
        copy.start()
        pack_copies.append(copy)
    own_plan = pltpu.make_async_copy(pack_ref, plan.at[0], plan_sem.at[0])
    own_plan.start()

    halo_copies = []
    loads[1].wait()
    loads[2].wait()
    for state, narrow in ((mom, mom_narrow), (sec, sec_narrow)):
        for j in range(capacity):
            narrow[j] = state[j].astype(jnp.bfloat16)
    right, left = h + 1 < 2 * levels, h > 0
    for i, (narrow, halo) in enumerate(((mom_narrow, mom_halo), (sec_narrow, sec_halo))):
        for side, condition, first, place, holder in (
            (0, right, capacity - holes, 0, h + 1), (1, left, 0, holes, h - 1),
        ):
            copy = pltpu.make_async_remote_copy(
                src_ref=narrow.at[pl.ds(first, holes)], dst_ref=halo.at[pl.ds(place, holes)],
                send_sem=halo_send.at[i, side], recv_sem=halo_recv.at[i, side],
                device_id=(f, holder), device_id_type=MESH,
            )
            when(condition, copy.start)
            comes = left if side == 0 else right
            halo_copies.append((condition, comes, copy))
    loads[3].wait()
    for r in range(tok_blocks.shape[0]):
        tok_blocks[r] = tok[:, r * block : (r + 1) * block]

    def prepare():
        own_plan.wait()
        plans = []
        for role in (1, 2, 3):
            pack_copies[role - 1].wait_recv()
            copy = pltpu.make_async_copy(packs.at[role - 1], plan.at[role], plan_sem.at[role])
            copy.start()
            plans.append(copy)
        for copy in plans:
            copy.wait()

    def finish(role):
        for level in range(levels):
            for piece in range(PIECES):
                await_piece(1, role, level, other, piece)

    stores = []

    def store(src, dst):
        copy = pltpu.make_async_copy(src, dst, store_sem.at[len(stores)])
        copy.start()
        stores.append(copy)

    def store_hidden(role):
        first = pl.multiple_of(jnp.bitwise_xor(f, role) * (columns * block), block)
        store(hids[role], hidden_ref.at[:, pl.ds(first, columns * block)])

    def migrate():
        for condition, comes, copy in halo_copies:
            when(comes, copy.wait_recv)
        low = h * capacity

        def settle(j, carry):
            source = plan[0, 1, j]
            present = source >= 0
            place = source - low
            local = jnp.logical_and(place >= 0, place < capacity)
            inside = jnp.clip(place, 0, capacity - 1)
            beside = jnp.where(place < 0, place + holes, place - capacity + holes)
            beside = jnp.clip(beside, 0, 2 * holes - 1)
            zero = jnp.zeros((block, block), jnp.float32)
            cell = jnp.clip(source, 0, cells - 1)
            for state, moved, index, target in (
                (mas, own, cell, new_mas), (mom, mom_halo, beside, new_mom), (sec, sec_halo, beside, new_sec),
            ):
                value = jnp.where(local, state[inside], moved[index].astype(jnp.float32))
                target[j] = jnp.where(present, value, zero)
            return carry

        lax.fori_loop(0, capacity, settle, 0)
        store(new_mas, master_out)
        store(new_mom, moment_out)
        store(new_sec, second_out)

    parts = [columns * i // 4 for i in range(5)]
    extra = {10: [prepare, functools.partial(finish, 0), migrate]}
    for i in range(4):
        extra.setdefault(11 + i, []).append(functools.partial(compute, 0, parts[i], parts[i + 1]))
    extra[14].append(functools.partial(store_hidden, 0))
    waiting = sorted(extra)
    for key, role, dz, piece in arrival_order(levels):
        while waiting and waiting[0] <= key:
            for act in extra[waiting.pop(0)]:
                act()
        handle(role, dz, piece)
    for slot in waiting:
        for act in extra[slot]:
            act()
    for role in (1, 2, 3):
        finish(role)
        compute(role, 0, columns)
        store_hidden(role)

    for condition, copy in sent:
        when(condition, copy.wait_send)
    for copy in pack_copies:
        copy.wait_send()
    for condition, comes, copy in halo_copies:
        when(condition, copy.wait_send)
    for copy in stores:
        copy.wait()


def on_device_kernel(tokens, master_old, moment_old, second_old, old_cell, new_cell, regrown, new_rows):
    capacity, block = master_old.shape[0], master_old.shape[1]
    columns, nonzero = old_cell.shape
    width, ways = lax.axis_size("dp"), lax.axis_size("fsdp")
    levels, cells, slots = width // 2, width * capacity, columns * nonzero
    holes = cells - slots
    listed = jnp.where(regrown == 0, old_cell, cells).reshape(1, -1)
    source = sources(old_cell, new_cell, regrown, capacity).reshape(1, -1)
    lanes = 128
    pack = jnp.concatenate(
        [
            jnp.pad(listed, ((0, 0), (0, lanes - slots))),
            jnp.pad(source, ((0, 6), (0, lanes - capacity))),
        ],
        axis=0,
    )
    token_count = tokens.shape[0]
    bf, f32 = jnp.bfloat16, jnp.float32
    any_space = pl.BlockSpec(memory_space=pl.ANY)
    state = pltpu.VMEM((capacity, block, block), f32)
    narrow = pltpu.VMEM((capacity, block, block), bf)
    halo = pltpu.VMEM((2 * holes, block, block), bf)
    out_state = jax.ShapeDtypeStruct(master_old.shape, f32)
    return pl.pallas_call(
        functools.partial(kernel, levels, holes, columns, nonzero),
        out_shape=(
            jax.ShapeDtypeStruct((token_count, ways * columns * block), bf), out_state, out_state, out_state,
        ),
        in_specs=[
            pl.BlockSpec(memory_space=pltpu.VMEM), pl.BlockSpec(memory_space=pltpu.SMEM),
            any_space, any_space, any_space, any_space,
        ],
        out_specs=(any_space,) * 4,
        scratch_shapes=[pltpu.VMEM((cells + 1, block, block), bf)] * 4
        + [pltpu.VMEM((token_count, columns * block), bf)] * 4
        + [
            pltpu.VMEM(tokens.shape, bf),
            pltpu.VMEM((tokens.shape[1] // block, token_count, block), bf),
            state, state, state, narrow, narrow, halo, halo, state, state, state,
            pltpu.VMEM((3, 8, lanes), jnp.int32),
            pltpu.SMEM((4, 8, lanes), jnp.int32),
            pltpu.SemaphoreType.DMA((4,)),
            pltpu.SemaphoreType.DMA((7,)),
            pltpu.SemaphoreType.DMA((4,)),
            pltpu.SemaphoreType.DMA((3,)),
            pltpu.SemaphoreType.DMA((3,)),
            pltpu.SemaphoreType.DMA((2, 2)),
            pltpu.SemaphoreType.DMA((2, 2)),
            pltpu.SemaphoreType.DMA((5, 4, PIECES, levels)),
            pltpu.SemaphoreType.DMA((2, 4, PIECES, levels)),
        ],
        compiler_params=pltpu.CompilerParams(
            collective_id=0, has_side_effects=True, vmem_limit_bytes=50 * 1024 * 1024
        ),
        cost_estimate=pl.CostEstimate(
            flops=2 * token_count * ways * slots * block * block,
            bytes_accessed=30 * 1024 * 1024, transcendentals=0,
        ),
    )(pack, new_rows, tokens, master_old, moment_old, second_old)


def takes_kernel(mesh, slots, capacity):
    ways, width = mesh.shape["fsdp"], mesh.shape["dp"]
    holes = width * capacity - slots
    return ways == 4 and width % 2 == 0 and PIECES <= capacity and 0 < holes <= capacity and slots <= 128


def solution(mesh):
    def on_device(*args):
        slots, capacity = args[4].size, args[1].shape[0]
        chosen = on_device_kernel if takes_kernel(mesh, slots, capacity) else on_device_plain
        return chosen(*args)

    return jax.shard_map(
        on_device,
        mesh=mesh,
        in_specs=(
            P(("fsdp", "dp"), None),
            P(("fsdp", "dp"), None, None),
            P(("fsdp", "dp"), None, None),
            P(("fsdp", "dp"), None, None),
            P("fsdp", None),
            P("fsdp", None),
            P("fsdp", None),
            P(),
        ),
        out_specs=(
            P(("fsdp", "dp"), None),
            P(("fsdp", "dp"), None, None),
            P(("fsdp", "dp"), None, None),
            P(("fsdp", "dp"), None, None),
        ),
        check_vma=False,
    )
```

```python
import functools

import jax
import jax.numpy as jnp
from jax import lax
from jax.experimental import pallas as pl
from jax.experimental.pallas import tpu as pltpu
from jax.sharding import PartitionSpec as P

MESH = pl.DeviceIdType.MESH
PIECES = 3
X, Y, UP, DOWN, TWIN = range(5)


def passed_along(block, axis, distance):
    devices = range(lax.axis_size(axis))
    route = [(i - distance, i) for i in devices if i - distance in devices]
    return lax.ppermute(block, axis, route)


def sources(old_cell, new_cell, regrown, capacity):
    old_flat, new_flat = old_cell.reshape(-1), new_cell.reshape(-1)
    kept = jnp.where(regrown.reshape(-1) == 0, old_flat, -1)
    my_cells = lax.axis_index("dp") * capacity + jnp.arange(capacity, dtype=jnp.int32)
    matches = new_flat[None, :] == my_cells[:, None]
    return jnp.max(jnp.where(matches, kept[None, :], -1), axis=1)


def on_device_plain(tokens, master_old, moment_old, second_old, old_cell, new_cell, regrown, new_rows):
    capacity, block_size = master_old.shape[0], master_old.shape[1]
    column_count, nonzero_count = old_cell.shape
    width = lax.axis_size("dp")
    holes = width * capacity - column_count * nonzero_count
    farthest = min((holes + capacity - 1) // capacity, width - 1)
    holder = lax.axis_index("dp")
    source = sources(old_cell, new_cell, regrown, capacity)
    present = source >= 0
    source = jnp.maximum(source, 0)
    offset = holder - source // capacity
    candidate = jnp.where(offset > 0, 2 * offset - 1, jnp.where(offset < 0, -2 * offset, 0))
    pick_index = candidate * capacity + source % capacity
    shifts = [s for distance in range(1, farthest + 1) for s in (distance, -distance)]

    def settle(state):
        narrow = state.astype(jnp.bfloat16)
        pool = [state] + [passed_along(narrow, "dp", s).astype(jnp.float32) for s in shifts]
        chosen = jnp.take(jnp.concatenate(pool, axis=0), pick_index, axis=0, mode="clip")
        return jnp.where(present[:, None, None], chosen, jnp.float32(0.0))

    cells = lax.all_gather(master_old.astype(jnp.bfloat16), "dp", axis=0, tiled=True)
    panel = jnp.take(cells, old_cell.reshape(-1), axis=0)
    panel = jnp.where(regrown.reshape(-1)[:, None, None] == 0, panel, jnp.bfloat16(0))
    panel = panel.reshape(column_count, nonzero_count, block_size, block_size)
    panel = lax.all_gather(panel, "fsdp", axis=0, tiled=True)
    count, token_count = panel.shape[0], tokens.shape[0]
    token_blocks = tokens.reshape(token_count, tokens.shape[1] // block_size, block_size)
    picked = jnp.take(token_blocks, new_rows.reshape(-1), axis=1)
    picked = picked.reshape(token_count, count, nonzero_count, block_size)
    product = jnp.einsum("tcka,ckab->tcb", picked, panel, preferred_element_type=jnp.float32)
    hidden = product.reshape(token_count, count * block_size).astype(jnp.bfloat16)
    return hidden, settle(master_old), settle(moment_old), settle(second_old)


def onward(levels, z, role, dz, piece):
    steps = []
    if role == 0 or (role == 3 and piece < 2):
        steps += [(DOWN, z - 1, role)] if dz >= 0 and z > 0 else []
        steps += [(UP, z + 1, role)] if dz <= 0 and z < levels - 1 else []
    if role == 0:
        steps += [(X, z, 1), (Y, z, 2)]
    even = (z + dz) % 2 == 0
    if role == 2 and ((piece == 0 and dz == 0) or (piece == 2 and even)):
        steps.append((X, z, 3))
    if role == 1 and ((piece == 1 and dz == 0) or (piece == 2 and not even)):
        steps.append((Y, z, 3))
    return steps


def arrival_order(levels):
    others = [dz for dz in range(1 - levels, levels)]
    order = [(r, dz, p) for dz in sorted(others, key=abs) for p in range(PIECES) for r in range(4) if r or dz]
    order.sort(key=lambda k: abs(k[1]) + (k[0] in (1, 2)) + 2 * (k[0] == 3))
    best = None
    for _ in range(12):
        script = [(0, 0, p) for p in range(PIECES)] + order
        arrived, free = {}, {}
        clock, place = [0.0] * levels, [0] * levels
        while True:
            nexts = []
            for z in range(levels):
                while place[z] < len(script) and not 0 <= z + script[place[z]][1] < levels:
                    place[z] += 1
                if place[z] < len(script):
                    role, dz, piece = script[place[z]]
                    came = 0.0 if (role, dz) == (0, 0) else arrived.get((z, role, dz, piece))
                    if came is not None:
                        nexts.append((max(clock[z], came), z))
            if not nexts:
                break
            now, z = min(nexts)
            role, dz, piece = script[place[z]]
            place[z] += 1
            for way, there, role_there in onward(levels, z, role, dz, piece):
                now += 0.15
                free[z, way] = max(free.get((z, way), 0.0), now) + 3.3
                arrived[there, role_there, z + dz - there, piece] = free[z, way] + 1.0
            clock[z] = now + 0.15
        if best is None or max(clock) < best[0]:
            best = (max(clock), order)
        mean = {}
        for key in order:
            came = [arrived[z, key[0], key[1], key[2]] for z in range(levels) if 0 <= z + key[1] < levels]
            mean[key] = sum(came) / len(came)
        order = sorted(order, key=lambda k: (mean[k], k))
    return best[1]


def kernel(
    levels, holes, columns, nonzero,
    pack_ref, rows_ref, tokens_ref, master_ref, moment_ref, second_ref,
    hidden_ref, master_out, moment_out, second_out,
    own, side_x, side_y, corner, hid0, hid1, hid2, hid3,
    tok, tok_blocks, mas, mom, sec, mom_narrow, sec_narrow, mom_halo, sec_halo,
    new_mas, new_mom, new_sec, packs, plan,
    load_sem, store_sem, plan_sem, pack_send, pack_recv, halo_send, halo_recv, send_sem, recv_sem,
):
    f, h = lax.axis_index("fsdp"), lax.axis_index("dp")
    z, core = h // 2, lax.rem(h, 2)
    capacity, block = mas.shape[0], mas.shape[1]
    cells = 2 * levels * capacity
    cuts = [capacity * i // PIECES for i in range(PIECES + 1)]
    groups = (own, side_x, side_y, corner)
    hids = (hid0, hid1, hid2, hid3)

    loads = [
        pltpu.make_async_copy(src, dst, load_sem.at[i])
        for i, (src, dst) in enumerate(
            [(master_ref, mas), (moment_ref, mom), (second_ref, sec), (tokens_ref, tok)]
        )
    ]
    for copy in loads:
        copy.start()

    barrier = pltpu.get_barrier_semaphore()

    def at(role, level, which):
        return (jnp.bitwise_xor(f, role), level * 2 + which)

    def greet(device):
        pl.semaphore_signal(barrier, inc=1, device_id=device, device_id_type=MESH)

    up, down = z + 1 < levels, z > 0
    other = 1 - core
    crossing = jnp.where(core == 1, up, down)
    cross_level = jnp.where(core == 1, z + 1, z - 1)

    for group in groups:
        group[cells] = jnp.zeros((block, block), jnp.bfloat16)
    mom_halo[...] = jnp.zeros_like(mom_halo)
    sec_halo[...] = jnp.zeros_like(sec_halo)

    for role in (1, 2, 3):
        greet(at(role, z, core))
    greet(at(0, z, other))

    @pl.when(up)
    def _():
        greet(at(0, z + 1, core))

    @pl.when(down)
    def _():
        greet(at(0, z - 1, core))

    @pl.when(crossing)
    def _():
        greet(at(0, cross_level, other))

    loads[0].wait()
    for j in range(capacity):
        own[h * capacity + j] = mas[j].astype(jnp.bfloat16)
    pl.semaphore_wait(barrier, 4 + up.astype(jnp.int32) + down.astype(jnp.int32) + crossing.astype(jnp.int32))

    sent = []

    def piece_ref(role, level, which, piece):
        first = (level * 2 + which) * capacity + cuts[piece]
        return groups[role].at[pl.ds(first, cuts[piece + 1] - cuts[piece])]

    def when(condition, act):
        if condition is True:
            act()
        else:
            pl.when(condition)(act)

    def send(condition, way, role, level, piece):
        target = {
            X: lambda: at(1, z, core), Y: lambda: at(2, z, core),
            UP: lambda: at(0, z + 1, core), DOWN: lambda: at(0, z - 1, core),
            TWIN: lambda: at(0, z, other),
        }[way]()
        there = role ^ {X: 1, Y: 2}.get(way, 0)
        copy = pltpu.make_async_remote_copy(
            src_ref=piece_ref(role, level, core, piece),
            dst_ref=piece_ref(there, level, core, piece),
            send_sem=send_sem.at[way, role, piece, level],
            recv_sem=recv_sem.at[1 if way == TWIN else 0, there, piece, level],
            device_id=target,
            device_id_type=MESH,
        )
        when(condition, copy.start)
        sent.append((condition, copy))

    def await_piece(lane, role, level, which, piece):
        part = piece_ref(role, level, which, piece)
        pltpu.make_async_remote_copy(
            src_ref=part, dst_ref=part, send_sem=send_sem.at[0, 0, 0, 0],
            recv_sem=recv_sem.at[lane, role, piece, level],
            device_id=at(0, z, other), device_id_type=MESH,
        ).wait_recv()

    def both(a, b):
        if a is True:
            return b
        return jnp.logical_and(a, b)

    def handle(role, dz, piece):
        level = z + dz
        if dz == 0:
            here = True
        else:
            here = level < levels if dz > 0 else level >= 0
        if (role, dz) != (0, 0):
            when(here, lambda: await_piece(0, role, level, core, piece))
        even = lax.rem(level + 2 * levels, 2) == 0
        if role == 0 or (role == 3 and piece < 2):
            if dz >= 0:
                send(both(here, down), DOWN, role, level, piece)
            if dz <= 0:
                send(both(here, up), UP, role, level, piece)
        if role == 0:
            send(here, X, role, level, piece)
            send(here, Y, role, level, piece)
        if role == 2:
            if piece == 0 and dz == 0:
                send(here, X, role, level, piece)
            if piece == 2:
                send(both(here, even), X, role, level, piece)
        if role == 1:
            if piece == 1 and dz == 0:
                send(here, Y, role, level, piece)
            if piece == 2:
                send(both(here, jnp.logical_not(even)), Y, role, level, piece)
        send(here, TWIN, role, level, piece)

    def compute(role, first, last):
        group, hid = groups[role], hids[role]
        base = jnp.bitwise_xor(f, role) * columns
        for c in range(first, last):
            left = [tok_blocks[rows_ref[k, base + c]] for k in range(nonzero)]
            right = [group[plan[role, k, c]] for k in range(nonzero)]
            total = jnp.dot(
                jnp.concatenate(left, axis=1), jnp.concatenate(right, axis=0),
                preferred_element_type=jnp.float32,
            )
            hid[:, c * block : (c + 1) * block] = total.astype(jnp.bfloat16)

    for piece in range(PIECES):
        handle(0, 0, piece)

    pack_copies = []
    for role in (1, 2, 3):
        copy = pltpu.make_async_remote_copy(
            src_ref=pack_ref, dst_ref=packs.at[role - 1],
            send_sem=pack_send.at[role - 1], recv_sem=pack_recv.at[role - 1],
            device_id=at(role, z, core), device_id_type=MESH,
        )
        copy.start()
        pack_copies.append(copy)
    own_plan = pltpu.make_async_copy(pack_ref, plan.at[0], plan_sem.at[0])
    own_plan.start()

    halo_copies = []
    loads[1].wait()
    loads[2].wait()
    for state, narrow in ((mom, mom_narrow), (sec, sec_narrow)):
        for j in range(capacity):
            narrow[j] = state[j].astype(jnp.bfloat16)
    right, left = h + 1 < 2 * levels, h > 0
    for i, (narrow, halo) in enumerate(((mom_narrow, mom_halo), (sec_narrow, sec_halo))):
        for side, condition, first, place, holder in (
            (0, right, capacity - holes, 0, h + 1), (1, left, 0, holes, h - 1),
        ):
            copy = pltpu.make_async_remote_copy(
                src_ref=narrow.at[pl.ds(first, holes)], dst_ref=halo.at[pl.ds(place, holes)],
                send_sem=halo_send.at[i, side], recv_sem=halo_recv.at[i, side],
                device_id=(f, holder), device_id_type=MESH,
            )
            when(condition, copy.start)
            comes = left if side == 0 else right
            halo_copies.append((condition, comes, copy))
    loads[3].wait()
    for r in range(tok_blocks.shape[0]):
        tok_blocks[r] = tok[:, r * block : (r + 1) * block]

    def prepare():
        own_plan.wait()
        plans = []
        for role in (1, 2, 3):
            pack_copies[role - 1].wait_recv()
            copy = pltpu.make_async_copy(packs.at[role - 1], plan.at[role], plan_sem.at[role])
            copy.start()
            plans.append(copy)
        for copy in plans:
            copy.wait()

    def finish(role):
        for level in range(levels):
            for piece in range(PIECES):
                await_piece(1, role, level, other, piece)

    stores = []

    def store(src, dst):
        copy = pltpu.make_async_copy(src, dst, store_sem.at[len(stores)])
        copy.start()
        stores.append(copy)

    def store_hidden(role):
        first = pl.multiple_of(jnp.bitwise_xor(f, role) * (columns * block), block)
        store(hids[role], hidden_ref.at[:, pl.ds(first, columns * block)])

    def migrate():
        for condition, comes, copy in halo_copies:
            when(comes, copy.wait_recv)
        low = h * capacity

        def settle(j, carry):
            source = jnp.int32(cells)
            for d in range(holes + 1):
                slot = low + j - d
                inside = jnp.clip(slot, 0, columns * nonzero - 1)
                c, k = inside // nonzero, lax.rem(inside, nonzero)
                match = jnp.logical_and(slot == inside, plan[0, nonzero + k, c] == low + j)
                source = jnp.where(match, plan[0, k, c], source)
            present = source < cells
            place = source - low
            local = jnp.logical_and(place >= 0, place < capacity)
            inside = jnp.clip(place, 0, capacity - 1)
            beside = jnp.where(place < 0, place + holes, place - capacity + holes)
            beside = jnp.clip(beside, 0, 2 * holes - 1)
            zero = jnp.zeros((block, block), jnp.float32)
            cell = jnp.clip(source, 0, cells - 1)
            for state, moved, index, target in (
                (mas, own, cell, new_mas), (mom, mom_halo, beside, new_mom), (sec, sec_halo, beside, new_sec),
            ):
                value = jnp.where(local, state[inside], moved[index].astype(jnp.float32))
                target[j] = jnp.where(present, value, zero)
            return carry

        lax.fori_loop(0, capacity, settle, 0)
        store(new_mas, master_out)
        store(new_mom, moment_out)
        store(new_sec, second_out)

    parts = [columns * i // 4 for i in range(5)]
    order = arrival_order(levels)
    last = {role: max(i for i, key in enumerate(order) if key[0] == role) for role in range(4)}
    todo = []
    for i, key in enumerate(order):
        handle(*key)
        if todo:
            todo.pop(0)()
        for role in range(4):
            if last[role] == i:
                if role == 0:
                    todo += [prepare]
                todo += [functools.partial(finish, role)]
                todo += [functools.partial(compute, role, parts[n], parts[n + 1]) for n in range(4)]
                todo += [functools.partial(store_hidden, role)]
                if role == 0:
                    todo += [migrate]
    for act in todo:
        act()

    for condition, copy in sent:
        when(condition, copy.wait_send)
    for copy in pack_copies:
        copy.wait_send()
    for condition, comes, copy in halo_copies:
        when(condition, copy.wait_send)
    for copy in stores:
        copy.wait()


def on_device_kernel(tokens, master_old, moment_old, second_old, old_cell, new_cell, regrown, new_rows):
    capacity, block = master_old.shape[0], master_old.shape[1]
    columns, nonzero = old_cell.shape
    width, ways = lax.axis_size("dp"), lax.axis_size("fsdp")
    levels, cells, slots = width // 2, width * capacity, columns * nonzero
    holes = cells - slots
    lanes = 128
    listed = jnp.where(regrown == 0, old_cell, cells).T
    pack = jnp.concatenate([listed, new_cell.T], axis=0)
    pack = jnp.pad(pack, ((0, 8 - 2 * nonzero), (0, lanes - columns)))
    token_count = tokens.shape[0]
    bf, f32 = jnp.bfloat16, jnp.float32
    any_space = pl.BlockSpec(memory_space=pl.ANY)
    state = pltpu.VMEM((capacity, block, block), f32)
    narrow = pltpu.VMEM((capacity, block, block), bf)
    halo = pltpu.VMEM((2 * holes, block, block), bf)
    out_state = jax.ShapeDtypeStruct(master_old.shape, f32)
    return pl.pallas_call(
        functools.partial(kernel, levels, holes, columns, nonzero),
        out_shape=(
            jax.ShapeDtypeStruct((token_count, ways * columns * block), bf), out_state, out_state, out_state,
        ),
        in_specs=[
            pl.BlockSpec(memory_space=pltpu.VMEM), pl.BlockSpec(memory_space=pltpu.SMEM),
            any_space, any_space, any_space, any_space,
        ],
        out_specs=(any_space,) * 4,
        scratch_shapes=[pltpu.VMEM((cells + 1, block, block), bf)] * 4
        + [pltpu.VMEM((token_count, columns * block), bf)] * 4
        + [
            pltpu.VMEM(tokens.shape, bf),
            pltpu.VMEM((tokens.shape[1] // block, token_count, block), bf),
            state, state, state, narrow, narrow, halo, halo, state, state, state,
            pltpu.VMEM((3, 8, lanes), jnp.int32),
            pltpu.SMEM((4, 8, lanes), jnp.int32),
            pltpu.SemaphoreType.DMA((4,)),
            pltpu.SemaphoreType.DMA((7,)),
            pltpu.SemaphoreType.DMA((4,)),
            pltpu.SemaphoreType.DMA((3,)),
            pltpu.SemaphoreType.DMA((3,)),
            pltpu.SemaphoreType.DMA((2, 2)),
            pltpu.SemaphoreType.DMA((2, 2)),
            pltpu.SemaphoreType.DMA((5, 4, PIECES, levels)),
            pltpu.SemaphoreType.DMA((2, 4, PIECES, levels)),
        ],
        compiler_params=pltpu.CompilerParams(
            collective_id=0, has_side_effects=True, vmem_limit_bytes=60 * 1024 * 1024
        ),
        cost_estimate=pl.CostEstimate(
            flops=2 * token_count * ways * slots * block * block,
            bytes_accessed=30 * 1024 * 1024, transcendentals=0,
        ),
    )(pack, new_rows.T, tokens, master_old, moment_old, second_old)


def takes_kernel(mesh, slots, capacity):
    ways, width = mesh.shape["fsdp"], mesh.shape["dp"]
    holes = width * capacity - slots
    return ways == 4 and width % 2 == 0 and PIECES <= capacity and 0 < holes <= capacity and slots <= 512


def solution(mesh):
    def on_device(*args):
        slots, capacity = args[4].size, args[1].shape[0]
        chosen = on_device_kernel if takes_kernel(mesh, slots, capacity) else on_device_plain
        return chosen(*args)

    return jax.shard_map(
        on_device,
        mesh=mesh,
        in_specs=(
            P(("fsdp", "dp"), None),
            P(("fsdp", "dp"), None, None),
            P(("fsdp", "dp"), None, None),
            P(("fsdp", "dp"), None, None),
            P("fsdp", None),
            P("fsdp", None),
            P("fsdp", None),
            P(),
        ),
        out_specs=(
            P(("fsdp", "dp"), None),
            P(("fsdp", "dp"), None, None),
            P(("fsdp", "dp"), None, None),
            P(("fsdp", "dp"), None, None),
        ),
        check_vma=False,
    )
```

```python
import functools

import jax
import jax.numpy as jnp
from jax import lax
from jax.experimental import pallas as pl
from jax.experimental.pallas import tpu as pltpu
from jax.sharding import PartitionSpec as P

MESH = pl.DeviceIdType.MESH
PIECES = 4
X, Y, UP, DOWN, TWIN = range(5)
KERNEL_VMEM = 105 * 1024 * 1024 // 2
LAST_VMEM = 24 * 1024 * 1024


def passed_along(block, axis, distance):
    devices = range(lax.axis_size(axis))
    route = [(i - distance, i) for i in devices if i - distance in devices]
    return lax.ppermute(block, axis, route)


def sources(old_cell, new_cell, regrown, capacity):
    old_flat, new_flat = old_cell.reshape(-1), new_cell.reshape(-1)
    kept = jnp.where(regrown.reshape(-1) == 0, old_flat, -1)
    my_cells = lax.axis_index("dp") * capacity + jnp.arange(capacity, dtype=jnp.int32)
    matches = new_flat[None, :] == my_cells[:, None]
    return jnp.max(jnp.where(matches, kept[None, :], -1), axis=1)


def on_device_plain(tokens, master_old, moment_old, second_old, old_cell, new_cell, regrown, new_rows):
    capacity, block_size = master_old.shape[0], master_old.shape[1]
    column_count, nonzero_count = old_cell.shape
    width = lax.axis_size("dp")
    holes = width * capacity - column_count * nonzero_count
    farthest = min((holes + capacity - 1) // capacity, width - 1)
    holder = lax.axis_index("dp")
    source = sources(old_cell, new_cell, regrown, capacity)
    present = source >= 0
    source = jnp.maximum(source, 0)
    offset = holder - source // capacity
    candidate = jnp.where(offset > 0, 2 * offset - 1, jnp.where(offset < 0, -2 * offset, 0))
    pick_index = candidate * capacity + source % capacity
    shifts = [s for distance in range(1, farthest + 1) for s in (distance, -distance)]

    def settle(state):
        narrow = state.astype(jnp.bfloat16)
        pool = [state] + [passed_along(narrow, "dp", s).astype(jnp.float32) for s in shifts]
        chosen = jnp.take(jnp.concatenate(pool, axis=0), pick_index, axis=0, mode="clip")
        return jnp.where(present[:, None, None], chosen, jnp.float32(0.0))

    cells = lax.all_gather(master_old.astype(jnp.bfloat16), "dp", axis=0, tiled=True)
    panel = jnp.take(cells, old_cell.reshape(-1), axis=0)
    panel = jnp.where(regrown.reshape(-1)[:, None, None] == 0, panel, jnp.bfloat16(0))
    panel = panel.reshape(column_count, nonzero_count, block_size, block_size)
    panel = lax.all_gather(panel, "fsdp", axis=0, tiled=True)
    count, token_count = panel.shape[0], tokens.shape[0]
    token_blocks = tokens.reshape(token_count, tokens.shape[1] // block_size, block_size)
    picked = jnp.take(token_blocks, new_rows.reshape(-1), axis=1)
    picked = picked.reshape(token_count, count, nonzero_count, block_size)
    product = jnp.einsum("tcka,ckab->tcb", picked, panel, preferred_element_type=jnp.float32)
    hidden = product.reshape(token_count, count * block_size).astype(jnp.bfloat16)
    return hidden, settle(master_old), settle(moment_old), settle(second_old)


def onward(levels, z, role, dz, piece):
    steps = []
    if role == 0 or (role == 3 and piece < 2):
        steps += [(DOWN, z - 1, role)] if dz >= 0 and z > 0 else []
        steps += [(UP, z + 1, role)] if dz <= 0 and z < levels - 1 else []
    if role == 0:
        steps += [(X, z, 1), (Y, z, 2)]
    even = (z + dz) % 2 == 0
    if role == 2 and ((piece == 0 and dz == 0) or piece == (2 if even else 3)):
        steps.append((X, z, 3))
    if role == 1 and ((piece == 1 and dz == 0) or piece == (3 if even else 2)):
        steps.append((Y, z, 3))
    return steps


def cuts_of(capacity):
    return [-(-capacity * i // PIECES) for i in range(PIECES + 1)]


def arrival_order(levels, capacity):
    others = [dz for dz in range(1 - levels, levels)]
    cuts = cuts_of(capacity)
    order = [(r, dz, p) for dz in sorted(others, key=abs) for p in range(PIECES) for r in range(4) if r or dz]
    order.sort(key=lambda k: abs(k[1]) + (k[0] in (1, 2)) + 2 * (k[0] == 3))
    best = None
    for _ in range(12):
        script = [(0, 0, p) for p in range(PIECES)] + order
        arrived, free = {}, {}
        clock, place = [0.0] * levels, [0] * levels
        while True:
            nexts = []
            for z in range(levels):
                while place[z] < len(script) and not 0 <= z + script[place[z]][1] < levels:
                    place[z] += 1
                if place[z] < len(script):
                    role, dz, piece = script[place[z]]
                    came = 0.0 if (role, dz) == (0, 0) else arrived.get((z, role, dz, piece))
                    if came is not None:
                        nexts.append((max(clock[z], came), z))
            if not nexts:
                break
            now, z = min(nexts)
            role, dz, piece = script[place[z]]
            place[z] += 1
            for way, there, role_there in onward(levels, z, role, dz, piece):
                now += 0.15
                free[z, way] = max(free.get((z, way), 0.0), now) + 0.66 * (cuts[piece + 1] - cuts[piece])
                arrived[there, role_there, z + dz - there, piece] = free[z, way] + 1.0
            clock[z] = now + 0.15
        if best is None or max(clock) < best[0]:
            best = (max(clock), order)
        mean = {}
        for key in order:
            came = [arrived[z, key[0], key[1], key[2]] for z in range(levels) if 0 <= z + key[1] < levels]
            mean[key] = sum(came) / len(came)
        order = sorted(order, key=lambda k: (mean[k], k))
    return best[1]


def multiply(tok_blocks, rows_ref, base, group, plan, at, hid, first, last, nonzero):
    block = group.shape[1]
    for c in range(first, last):
        left = [tok_blocks[rows_ref[k, base + c]] for k in range(nonzero)]
        right = [group[plan[(*at, k, c)]] for k in range(nonzero)]
        total = jnp.dot(
            jnp.concatenate(left, axis=1), jnp.concatenate(right, axis=0),
            preferred_element_type=jnp.float32,
        )
        hid[:, c * block : (c + 1) * block] = total.astype(jnp.bfloat16)


def last_kernel(
    columns, nonzero,
    corner, hid0, hid1, hid2, new_mas, new_mom, new_sec, tok_blocks, packs, rows_ref,
    hidden_ref, master_out, moment_out, second_out,
    hid3, plan, plan_sem, store_sem,
):
    f = lax.axis_index("fsdp")
    block = corner.shape[1]
    listing = pltpu.make_async_copy(packs.at[2], plan, plan_sem)
    listing.start()
    stores = []

    def store(src, dst):
        copy = pltpu.make_async_copy(src, dst, store_sem.at[len(stores)])
        copy.start()
        stores.append(copy)

    def hidden_part(role, first, last):
        start = pl.multiple_of((jnp.bitwise_xor(f, role) * columns + first) * block, block)
        return hidden_ref.at[:, pl.ds(start, (last - first) * block)]

    for role, hid in enumerate((hid0, hid1, hid2)):
        store(hid, hidden_part(role, 0, columns))
    store(new_mas, master_out)
    store(new_mom, moment_out)
    store(new_sec, second_out)
    listing.wait()
    parts = [columns * i // 4 for i in range(5)]
    for first, last in zip(parts, parts[1:]):
        multiply(tok_blocks, rows_ref, jnp.bitwise_xor(f, 3) * columns, corner, plan, (), hid3, first, last, nonzero)
        store(hid3.at[:, pl.ds(first * block, (last - first) * block)], hidden_part(3, first, last))
    for copy in stores:
        copy.wait()


def kernel(
    levels, holes, columns, nonzero,
    pack_ref, rows_ref, tokens_ref, master_ref, moment_ref, second_ref,
    corner, hid0, hid1, hid2, new_mas, new_mom, new_sec, tok_blocks, packs,
    own, side_x, side_y, tok, mas, mom, sec, mom_narrow, sec_narrow, mom_halo, sec_halo, plan,
    load_sem, plan_sem, pack_send, pack_recv, halo_send, halo_recv, send_sem, recv_sem,
):
    f, h = lax.axis_index("fsdp"), lax.axis_index("dp")
    z, core = h // 2, lax.rem(h, 2)
    capacity, block = mas.shape[0], mas.shape[1]
    cells = 2 * levels * capacity
    cuts = cuts_of(capacity)
    groups = (own, side_x, side_y, corner)
    hids = (hid0, hid1, hid2)

    loads = [
        pltpu.make_async_copy(src, dst, load_sem.at[i])
        for i, (src, dst) in enumerate(
            [(master_ref, mas), (moment_ref, mom), (second_ref, sec), (tokens_ref, tok)]
        )
    ]
    for copy in loads:
        copy.start()

    barrier = pltpu.get_barrier_semaphore()

    def at(role, level, which):
        return (jnp.bitwise_xor(f, role), level * 2 + which)

    def greet(device):
        pl.semaphore_signal(barrier, inc=1, device_id=device, device_id_type=MESH)

    up, down = z + 1 < levels, z > 0
    other = 1 - core
    crossing = jnp.where(core == 1, up, down)
    cross_level = jnp.where(core == 1, z + 1, z - 1)

    for group in groups:
        group[cells] = jnp.zeros((block, block), jnp.bfloat16)
    mom_halo[...] = jnp.zeros_like(mom_halo)
    sec_halo[...] = jnp.zeros_like(sec_halo)

    for role in (1, 2, 3):
        greet(at(role, z, core))
    greet(at(0, z, other))

    @pl.when(up)
    def _():
        greet(at(0, z + 1, core))

    @pl.when(down)
    def _():
        greet(at(0, z - 1, core))

    @pl.when(crossing)
    def _():
        greet(at(0, cross_level, other))

    loads[0].wait()
    for j in range(capacity):
        own[h * capacity + j] = mas[j].astype(jnp.bfloat16)
    pl.semaphore_wait(barrier, 4 + up.astype(jnp.int32) + down.astype(jnp.int32) + crossing.astype(jnp.int32))

    sent = []

    def piece_ref(role, level, which, piece):
        first = (level * 2 + which) * capacity + cuts[piece]
        return groups[role].at[pl.ds(first, cuts[piece + 1] - cuts[piece])]

    def when(condition, act):
        if condition is True:
            act()
        else:
            pl.when(condition)(act)

    def send(condition, way, role, level, piece):
        target = {
            X: lambda: at(1, z, core), Y: lambda: at(2, z, core),
            UP: lambda: at(0, z + 1, core), DOWN: lambda: at(0, z - 1, core),
            TWIN: lambda: at(0, z, other),
        }[way]()
        there = role ^ {X: 1, Y: 2}.get(way, 0)
        copy = pltpu.make_async_remote_copy(
            src_ref=piece_ref(role, level, core, piece),
            dst_ref=piece_ref(there, level, core, piece),
            send_sem=send_sem.at[way, role, piece, level],
            recv_sem=recv_sem.at[1 if way == TWIN else 0, there, piece, level],
            device_id=target,
            device_id_type=MESH,
        )
        when(condition, copy.start)
        sent.append((condition, copy))

    def await_piece(lane, role, level, which, piece):
        part = piece_ref(role, level, which, piece)
        pltpu.make_async_remote_copy(
            src_ref=part, dst_ref=part, send_sem=send_sem.at[0, 0, 0, 0],
            recv_sem=recv_sem.at[lane, role, piece, level],
            device_id=at(0, z, other), device_id_type=MESH,
        ).wait_recv()

    def both(a, b):
        if a is True:
            return b
        return jnp.logical_and(a, b)

    def handle(role, dz, piece):
        level = z + dz
        if dz == 0:
            here = True
        else:
            here = level < levels if dz > 0 else level >= 0
        if (role, dz) != (0, 0):
            when(here, lambda: await_piece(0, role, level, core, piece))
        even = lax.rem(level + 2 * levels, 2) == 0
        if role == 0 or (role == 3 and piece < 2):
            if dz >= 0:
                send(both(here, down), DOWN, role, level, piece)
            if dz <= 0:
                send(both(here, up), UP, role, level, piece)
        if role == 0:
            send(here, X, role, level, piece)
            send(here, Y, role, level, piece)
        if role == 2:
            if piece == 0 and dz == 0:
                send(here, X, role, level, piece)
            if piece >= 2:
                send(both(here, even if piece == 2 else jnp.logical_not(even)), X, role, level, piece)
        if role == 1:
            if piece == 1 and dz == 0:
                send(here, Y, role, level, piece)
            if piece >= 2:
                send(both(here, even if piece == 3 else jnp.logical_not(even)), Y, role, level, piece)
        send(here, TWIN, role, level, piece)

    def compute(role, first, last):
        base = jnp.bitwise_xor(f, role) * columns
        multiply(tok_blocks, rows_ref, base, groups[role], plan, (role,), hids[role], first, last, nonzero)

    for piece in range(PIECES):
        handle(0, 0, piece)

    pack_copies = []
    for role in (1, 2, 3):
        copy = pltpu.make_async_remote_copy(
            src_ref=pack_ref, dst_ref=packs.at[role - 1],
            send_sem=pack_send.at[role - 1], recv_sem=pack_recv.at[role - 1],
            device_id=at(role, z, core), device_id_type=MESH,
        )
        copy.start()
        pack_copies.append(copy)
    own_plan = pltpu.make_async_copy(pack_ref, plan.at[0], plan_sem.at[0])
    own_plan.start()

    halo_copies = []
    right, left = h + 1 < 2 * levels, h > 0
    for i, (narrow, halo) in enumerate(((mom_narrow, mom_halo), (sec_narrow, sec_halo))):
        for side, condition, first, place, holder in (
            (0, right, capacity - holes, 0, h + 1), (1, left, 0, holes, h - 1),
        ):
            copy = pltpu.make_async_remote_copy(
                src_ref=narrow.at[pl.ds(first, holes)], dst_ref=halo.at[pl.ds(place, holes)],
                send_sem=halo_send.at[i, side], recv_sem=halo_recv.at[i, side],
                device_id=(f, holder), device_id_type=MESH,
            )
            halo_copies.append((condition, left if side == 0 else right, copy))

    def send_halo():
        for condition, comes, copy in halo_copies:
            when(condition, copy.start)

    loads[1].wait()
    loads[2].wait()
    for state, narrow in ((mom, mom_narrow), (sec, sec_narrow)):
        for j in range(capacity):
            narrow[j] = state[j].astype(jnp.bfloat16)
    loads[3].wait()
    for r in range(tok_blocks.shape[0]):
        tok_blocks[r] = tok[:, r * block : (r + 1) * block]

    def prepare():
        own_plan.wait()
        plans = []
        for role in (1, 2, 3):
            pack_copies[role - 1].wait_recv()
            copy = pltpu.make_async_copy(packs.at[role - 1], plan.at[role], plan_sem.at[role])
            copy.start()
            plans.append(copy)
        for copy in plans:
            copy.wait()

    def finish(role):
        for level in range(levels):
            for piece in range(PIECES):
                await_piece(1, role, level, other, piece)

    def migrate():
        for condition, comes, copy in halo_copies:
            when(comes, copy.wait_recv)
        low = h * capacity

        def settle(j, carry):
            source = jnp.int32(cells)
            for d in range(holes + 1):
                slot = low + j - d
                inside = jnp.clip(slot, 0, columns * nonzero - 1)
                c, k = inside // nonzero, lax.rem(inside, nonzero)
                match = jnp.logical_and(slot == inside, plan[0, nonzero + k, c] == low + j)
                source = jnp.where(match, plan[0, k, c], source)
            present = source < cells
            place = source - low
            local = jnp.logical_and(place >= 0, place < capacity)
            inside = jnp.clip(place, 0, capacity - 1)
            beside = jnp.where(place < 0, place + holes, place - capacity + holes)
            beside = jnp.clip(beside, 0, 2 * holes - 1)
            zero = jnp.zeros((block, block), jnp.float32)
            cell = jnp.clip(source, 0, cells - 1)
            for state, moved, index, target in (
                (mas, own, cell, new_mas), (mom, mom_halo, beside, new_mom), (sec, sec_halo, beside, new_sec),
            ):
                value = jnp.where(local, state[inside], moved[index].astype(jnp.float32))
                target[j] = jnp.where(present, value, zero)
            return carry

        lax.fori_loop(0, capacity, settle, 0)

    parts = [columns * i // 4 for i in range(5)]
    order = arrival_order(levels, capacity)
    last = {role: max(i for i, key in enumerate(order) if key[0] == role) for role in range(4)}
    todo = []
    for i, key in enumerate(order):
        handle(*key)
        if todo:
            todo.pop(0)()
        for role in range(3):
            if last[role] == i:
                todo += [send_halo, prepare] if role == 0 else []
                todo += [functools.partial(finish, role)]
                todo += [functools.partial(compute, role, parts[n], parts[n + 1]) for n in range(4)]
                todo += [migrate] if role == 0 else []
    for act in todo:
        act()
    finish(3)

    for condition, copy in sent:
        when(condition, copy.wait_send)
    for copy in pack_copies:
        copy.wait_send()
    for condition, comes, copy in halo_copies:
        when(condition, copy.wait_send)

def on_device_kernel(tokens, master_old, moment_old, second_old, old_cell, new_cell, regrown, new_rows):
    capacity, block = master_old.shape[0], master_old.shape[1]
    columns, nonzero = old_cell.shape
    width, ways = lax.axis_size("dp"), lax.axis_size("fsdp")
    levels, cells, slots = width // 2, width * capacity, columns * nonzero
    holes = cells - slots
    lanes = 128
    listed = jnp.where(regrown == 0, old_cell, cells).T
    pack = jnp.concatenate([listed, new_cell.T], axis=0)
    pack = jnp.pad(pack, ((0, 8 - 2 * nonzero), (0, lanes - columns)))
    token_count = tokens.shape[0]
    bf, f32, i32 = jnp.bfloat16, jnp.float32, jnp.int32
    any_space = pl.BlockSpec(memory_space=pl.ANY)
    vmem, smem = pl.BlockSpec(memory_space=pltpu.VMEM), pl.BlockSpec(memory_space=pltpu.SMEM)
    state = pltpu.VMEM((capacity, block, block), f32)
    narrow = pltpu.VMEM((capacity, block, block), bf)
    halo = pltpu.VMEM((2 * holes, block, block), bf)
    group = pltpu.VMEM((cells + 1, block, block), bf)
    hid = pltpu.VMEM((token_count, columns * block), bf)
    tok_blocks = pltpu.VMEM((tokens.shape[1] // block, token_count, block), bf)
    rows = new_rows.T
    flops = 2 * token_count * slots * block * block
    between = pl.pallas_call(
        functools.partial(kernel, levels, holes, columns, nonzero),
        out_shape=(group, hid, hid, hid, state, state, state, tok_blocks, pltpu.VMEM((3, 8, lanes), i32)),
        in_specs=[vmem, smem, any_space, any_space, any_space, any_space],
        out_specs=(vmem,) * 9,
        scratch_shapes=[
            group, group, group, pltpu.VMEM(tokens.shape, bf), state, state, state, narrow, narrow, halo, halo,
            pltpu.SMEM((4, 8, lanes), i32),
            pltpu.SemaphoreType.DMA((4,)),
            pltpu.SemaphoreType.DMA((4,)),
            pltpu.SemaphoreType.DMA((3,)),
            pltpu.SemaphoreType.DMA((3,)),
            pltpu.SemaphoreType.DMA((2, 2)),
            pltpu.SemaphoreType.DMA((2, 2)),
            pltpu.SemaphoreType.DMA((5, 4, PIECES, levels)),
            pltpu.SemaphoreType.DMA((2, 4, PIECES, levels)),
        ],
        compiler_params=pltpu.CompilerParams(
            collective_id=0, has_side_effects=True, vmem_limit_bytes=KERNEL_VMEM
        ),
        cost_estimate=pl.CostEstimate(
            flops=3 * flops, bytes_accessed=16 * 1024 * 1024, transcendentals=0
        ),
    )(pack, rows, tokens, master_old, moment_old, second_old)
    out_state = jax.ShapeDtypeStruct(master_old.shape, f32)
    return pl.pallas_call(
        functools.partial(last_kernel, columns, nonzero),
        out_shape=(
            jax.ShapeDtypeStruct((token_count, ways * columns * block), bf), out_state, out_state, out_state,
        ),
        in_specs=[vmem] * 9 + [smem],
        out_specs=(any_space,) * 4,
        scratch_shapes=[
            hid,
            pltpu.SMEM((8, lanes), i32),
            pltpu.SemaphoreType.DMA,
            pltpu.SemaphoreType.DMA((10,)),
        ],
        compiler_params=pltpu.CompilerParams(vmem_limit_bytes=LAST_VMEM),
        cost_estimate=pl.CostEstimate(flops=flops, bytes_accessed=8 * 1024 * 1024, transcendentals=0),
    )(*between, rows)


def takes_kernel(mesh, slots, capacity):
    ways, width = mesh.shape["fsdp"], mesh.shape["dp"]
    holes = width * capacity - slots
    return ways == 4 and width % 2 == 0 and PIECES <= capacity and 0 < holes <= capacity and slots <= 512


def solution(mesh):
    def on_device(*args):
        slots, capacity = args[4].size, args[1].shape[0]
        chosen = on_device_kernel if takes_kernel(mesh, slots, capacity) else on_device_plain
        return chosen(*args)

    return jax.shard_map(
        on_device,
        mesh=mesh,
        in_specs=(
            P(("fsdp", "dp"), None),
            P(("fsdp", "dp"), None, None),
            P(("fsdp", "dp"), None, None),
            P(("fsdp", "dp"), None, None),
            P("fsdp", None),
            P("fsdp", None),
            P("fsdp", None),
            P(),
        ),
        out_specs=(
            P(("fsdp", "dp"), None),
            P(("fsdp", "dp"), None, None),
            P(("fsdp", "dp"), None, None),
            P(("fsdp", "dp"), None, None),
        ),
        check_vma=False,
    )
```

```python
import functools

import jax
import jax.numpy as jnp
from jax import lax
from jax.experimental import pallas as pl
from jax.experimental.pallas import tpu as pltpu
from jax.sharding import PartitionSpec as P

MESH = pl.DeviceIdType.MESH
PIECES = 4
X, Y, UP, DOWN, TWIN = range(5)
KERNEL_VMEM = 105 * 1024 * 1024 // 2
LAST_VMEM = 24 * 1024 * 1024


def passed_along(block, axis, distance):
    devices = range(lax.axis_size(axis))
    route = [(i - distance, i) for i in devices if i - distance in devices]
    return lax.ppermute(block, axis, route)


def sources(old_cell, new_cell, regrown, capacity):
    old_flat, new_flat = old_cell.reshape(-1), new_cell.reshape(-1)
    kept = jnp.where(regrown.reshape(-1) == 0, old_flat, -1)
    my_cells = lax.axis_index("dp") * capacity + jnp.arange(capacity, dtype=jnp.int32)
    matches = new_flat[None, :] == my_cells[:, None]
    return jnp.max(jnp.where(matches, kept[None, :], -1), axis=1)


def on_device_plain(tokens, master_old, moment_old, second_old, old_cell, new_cell, regrown, new_rows):
    capacity, block_size = master_old.shape[0], master_old.shape[1]
    column_count, nonzero_count = old_cell.shape
    width = lax.axis_size("dp")
    holes = width * capacity - column_count * nonzero_count
    farthest = min((holes + capacity - 1) // capacity, width - 1)
    holder = lax.axis_index("dp")
    source = sources(old_cell, new_cell, regrown, capacity)
    present = source >= 0
    source = jnp.maximum(source, 0)
    offset = holder - source // capacity
    candidate = jnp.where(offset > 0, 2 * offset - 1, jnp.where(offset < 0, -2 * offset, 0))
    pick_index = candidate * capacity + source % capacity
    shifts = [s for distance in range(1, farthest + 1) for s in (distance, -distance)]

    def settle(state):
        narrow = state.astype(jnp.bfloat16)
        pool = [state] + [passed_along(narrow, "dp", s).astype(jnp.float32) for s in shifts]
        chosen = jnp.take(jnp.concatenate(pool, axis=0), pick_index, axis=0, mode="clip")
        return jnp.where(present[:, None, None], chosen, jnp.float32(0.0))

    cells = lax.all_gather(master_old.astype(jnp.bfloat16), "dp", axis=0, tiled=True)
    panel = jnp.take(cells, old_cell.reshape(-1), axis=0)
    panel = jnp.where(regrown.reshape(-1)[:, None, None] == 0, panel, jnp.bfloat16(0))
    panel = panel.reshape(column_count, nonzero_count, block_size, block_size)
    panel = lax.all_gather(panel, "fsdp", axis=0, tiled=True)
    count, token_count = panel.shape[0], tokens.shape[0]
    token_blocks = tokens.reshape(token_count, tokens.shape[1] // block_size, block_size)
    picked = jnp.take(token_blocks, new_rows.reshape(-1), axis=1)
    picked = picked.reshape(token_count, count, nonzero_count, block_size)
    product = jnp.einsum("tcka,ckab->tcb", picked, panel, preferred_element_type=jnp.float32)
    hidden = product.reshape(token_count, count * block_size).astype(jnp.bfloat16)
    return hidden, settle(master_old), settle(moment_old), settle(second_old)


def onward(levels, z, role, dz, piece):
    steps = []
    if role == 0 or (role == 3 and piece < 2):
        steps += [(DOWN, z - 1, role)] if dz >= 0 and z > 0 else []
        steps += [(UP, z + 1, role)] if dz <= 0 and z < levels - 1 else []
    if role == 0:
        steps += [(X, z, 1), (Y, z, 2)]
    even = (z + dz) % 2 == 0
    if role == 2 and ((piece == 0 and dz == 0) or piece == (2 if even else 3)):
        steps.append((X, z, 3))
    if role == 1 and ((piece == 1 and dz == 0) or piece == (3 if even else 2)):
        steps.append((Y, z, 3))
    return steps


def cuts_of(capacity):
    return [-(-capacity * i // PIECES) for i in range(PIECES + 1)]


def arrival_order(levels, capacity):
    others = [dz for dz in range(1 - levels, levels)]
    cuts = cuts_of(capacity)
    order = [(r, dz, p) for dz in sorted(others, key=abs) for p in range(PIECES) for r in range(4) if r or dz]
    order.sort(key=lambda k: abs(k[1]) + (k[0] in (1, 2)) + 2 * (k[0] == 3))
    best = None
    total = 0.66 * 5.2 * capacity
    for turn in range(14):
        script = [(0, 0, p) for p in range(PIECES)] + order
        arrived, free = {}, {}
        clock, place = [0.0] * levels, [0] * levels
        while True:
            nexts = []
            for z in range(levels):
                while place[z] < len(script) and not 0 <= z + script[place[z]][1] < levels:
                    place[z] += 1
                if place[z] < len(script):
                    role, dz, piece = script[place[z]]
                    came = 0.0 if (role, dz) == (0, 0) else arrived.get((z, role, dz, piece))
                    if came is not None:
                        nexts.append((max(clock[z], came), z))
            if not nexts:
                break
            now, z = min(nexts)
            role, dz, piece = script[place[z]]
            place[z] += 1
            for way, there, role_there in onward(levels, z, role, dz, piece):
                now += 0.15
                free[z, way] = max(free.get((z, way), 0.0), now) + 0.66 * (cuts[piece + 1] - cuts[piece])
                arrived[there, role_there, z + dz - there, piece] = free[z, way] + 1.0
            clock[z] = now + 0.15
        if turn >= 2 and (best is None or max(clock) < best[0]):
            best = (max(clock), order)
        mean = {}
        for key in order:
            came = [arrived[z, key[0], key[1], key[2]] for z in range(levels) if 0 <= z + key[1] < levels]
            held = 0.0
            if key[0] == 3:
                held = 0.87 if key[2] >= 2 else 0.4
            elif key[0] and key[2] >= 2:
                held = 0.68
            mean[key] = max(sum(came) / len(came), held * total)
        order = sorted(order, key=lambda k: (mean[k], k))
    return best[1]


def multiply(tok_blocks, rows_ref, base, group, plan, at, hid, first, last, nonzero):
    block = group.shape[1]
    for c in range(first, last):
        left = [tok_blocks[rows_ref[k, base + c]] for k in range(nonzero)]
        right = [group[plan[(*at, k, c)]] for k in range(nonzero)]
        total = jnp.dot(
            jnp.concatenate(left, axis=1), jnp.concatenate(right, axis=0),
            preferred_element_type=jnp.float32,
        )
        hid[:, c * block : (c + 1) * block] = total.astype(jnp.bfloat16)


def last_kernel(
    columns, nonzero,
    corner, hid0, hid1, hid2, new_mas, new_mom, new_sec, tok_blocks, packs, rows_ref,
    hidden_ref, master_out, moment_out, second_out,
    hid3, plan, plan_sem, store_sem,
):
    f = lax.axis_index("fsdp")
    block = corner.shape[1]
    listing = pltpu.make_async_copy(packs.at[2], plan, plan_sem)
    listing.start()
    stores = []

    def store(src, dst):
        copy = pltpu.make_async_copy(src, dst, store_sem.at[len(stores)])
        copy.start()
        stores.append(copy)

    def hidden_part(role, first, last):
        start = pl.multiple_of((jnp.bitwise_xor(f, role) * columns + first) * block, block)
        return hidden_ref.at[:, pl.ds(start, (last - first) * block)]

    for role, hid in enumerate((hid0, hid1, hid2)):
        store(hid, hidden_part(role, 0, columns))
    store(new_mas, master_out)
    store(new_mom, moment_out)
    store(new_sec, second_out)
    listing.wait()
    parts = [columns * i // 4 for i in range(5)]
    for first, last in zip(parts, parts[1:]):
        multiply(tok_blocks, rows_ref, jnp.bitwise_xor(f, 3) * columns, corner, plan, (), hid3, first, last, nonzero)
        store(hid3.at[:, pl.ds(first * block, (last - first) * block)], hidden_part(3, first, last))
    for copy in stores:
        copy.wait()


def kernel(
    levels, holes, columns, nonzero,
    pack_ref, rows_ref, tokens_ref, master_ref, moment_ref, second_ref,
    corner, hid0, hid1, hid2, new_mas, new_mom, new_sec, tok_blocks, packs,
    own, side_x, side_y, tok, mas, mom, sec, mom_narrow, sec_narrow, mom_halo, sec_halo, plan,
    load_sem, plan_sem, pack_send, pack_recv, halo_send, halo_recv, send_sem, recv_sem,
):
    f, h = lax.axis_index("fsdp"), lax.axis_index("dp")
    z, core = h // 2, lax.rem(h, 2)
    capacity, block = mas.shape[0], mas.shape[1]
    cells = 2 * levels * capacity
    cuts = cuts_of(capacity)
    groups = (own, side_x, side_y, corner)
    hids = (hid0, hid1, hid2)

    loads = [
        pltpu.make_async_copy(src, dst, load_sem.at[i])
        for i, (src, dst) in enumerate(
            [(master_ref, mas), (moment_ref, mom), (second_ref, sec), (tokens_ref, tok)]
        )
    ]
    for copy in loads:
        copy.start()

    barrier = pltpu.get_barrier_semaphore()

    def at(role, level, which):
        return (jnp.bitwise_xor(f, role), level * 2 + which)

    def greet(device):
        pl.semaphore_signal(barrier, inc=1, device_id=device, device_id_type=MESH)

    up, down = z + 1 < levels, z > 0
    other = 1 - core
    crossing = jnp.where(core == 1, up, down)
    cross_level = jnp.where(core == 1, z + 1, z - 1)

    for group in groups:
        group[cells] = jnp.zeros((block, block), jnp.bfloat16)
    mom_halo[...] = jnp.zeros_like(mom_halo)
    sec_halo[...] = jnp.zeros_like(sec_halo)

    for role in (1, 2, 3):
        greet(at(role, z, core))
    greet(at(0, z, other))

    @pl.when(up)
    def _():
        greet(at(0, z + 1, core))

    @pl.when(down)
    def _():
        greet(at(0, z - 1, core))

    @pl.when(crossing)
    def _():
        greet(at(0, cross_level, other))

    loads[0].wait()
    for j in range(capacity):
        own[h * capacity + j] = mas[j].astype(jnp.bfloat16)
    pl.semaphore_wait(barrier, 4 + up.astype(jnp.int32) + down.astype(jnp.int32) + crossing.astype(jnp.int32))

    sent = []

    def piece_ref(role, level, which, piece):
        first = (level * 2 + which) * capacity + cuts[piece]
        return groups[role].at[pl.ds(first, cuts[piece + 1] - cuts[piece])]

    def when(condition, act):
        if condition is True:
            act()
        else:
            pl.when(condition)(act)

    def send(condition, way, role, level, piece):
        target = {
            X: lambda: at(1, z, core), Y: lambda: at(2, z, core),
            UP: lambda: at(0, z + 1, core), DOWN: lambda: at(0, z - 1, core),
            TWIN: lambda: at(0, z, other),
        }[way]()
        there = role ^ {X: 1, Y: 2}.get(way, 0)
        copy = pltpu.make_async_remote_copy(
            src_ref=piece_ref(role, level, core, piece),
            dst_ref=piece_ref(there, level, core, piece),
            send_sem=send_sem.at[way, role, piece, level],
            recv_sem=recv_sem.at[1 if way == TWIN else 0, there, piece, level],
            device_id=target,
            device_id_type=MESH,
        )
        when(condition, copy.start)
        sent.append((condition, copy))

    def await_piece(lane, role, level, which, piece):
        part = piece_ref(role, level, which, piece)
        pltpu.make_async_remote_copy(
            src_ref=part, dst_ref=part, send_sem=send_sem.at[0, 0, 0, 0],
            recv_sem=recv_sem.at[lane, role, piece, level],
            device_id=at(0, z, other), device_id_type=MESH,
        ).wait_recv()

    def both(a, b):
        if a is True:
            return b
        return jnp.logical_and(a, b)

    def handle(role, dz, piece):
        level = z + dz
        if dz == 0:
            here = True
        else:
            here = level < levels if dz > 0 else level >= 0
        if (role, dz) != (0, 0):
            when(here, lambda: await_piece(0, role, level, core, piece))
        even = lax.rem(level + 2 * levels, 2) == 0
        if role == 0 or (role == 3 and piece < 2):
            if dz >= 0:
                send(both(here, down), DOWN, role, level, piece)
            if dz <= 0:
                send(both(here, up), UP, role, level, piece)
        if role == 0:
            send(here, X, role, level, piece)
            send(here, Y, role, level, piece)
        if role == 2:
            if piece == 0 and dz == 0:
                send(here, X, role, level, piece)
            if piece >= 2:
                send(both(here, even if piece == 2 else jnp.logical_not(even)), X, role, level, piece)
        if role == 1:
            if piece == 1 and dz == 0:
                send(here, Y, role, level, piece)
            if piece >= 2:
                send(both(here, even if piece == 3 else jnp.logical_not(even)), Y, role, level, piece)
        send(here, TWIN, role, level, piece)

    def compute(role, first, last):
        base = jnp.bitwise_xor(f, role) * columns
        multiply(tok_blocks, rows_ref, base, groups[role], plan, (role,), hids[role], first, last, nonzero)

    for piece in range(PIECES):
        handle(0, 0, piece)

    pack_copies = []
    for role in (1, 2, 3):
        copy = pltpu.make_async_remote_copy(
            src_ref=pack_ref, dst_ref=packs.at[role - 1],
            send_sem=pack_send.at[role - 1], recv_sem=pack_recv.at[role - 1],
            device_id=at(role, z, core), device_id_type=MESH,
        )
        copy.start()
        pack_copies.append(copy)
    own_plan = pltpu.make_async_copy(pack_ref, plan.at[0], plan_sem.at[0])
    own_plan.start()

    halo_copies = []
    right, left = h + 1 < 2 * levels, h > 0
    for i, (narrow, halo) in enumerate(((mom_narrow, mom_halo), (sec_narrow, sec_halo))):
        for side, condition, first, place, holder in (
            (0, right, capacity - holes, 0, h + 1), (1, left, 0, holes, h - 1),
        ):
            copy = pltpu.make_async_remote_copy(
                src_ref=narrow.at[pl.ds(first, holes)], dst_ref=halo.at[pl.ds(place, holes)],
                send_sem=halo_send.at[i, side], recv_sem=halo_recv.at[i, side],
                device_id=(f, holder), device_id_type=MESH,
            )
            halo_copies.append((condition, left if side == 0 else right, copy))

    def send_halo():
        for condition, comes, copy in halo_copies:
            when(condition, copy.start)

    loads[1].wait()
    loads[2].wait()
    for state, narrow in ((mom, mom_narrow), (sec, sec_narrow)):
        for j in range(capacity):
            narrow[j] = state[j].astype(jnp.bfloat16)
    loads[3].wait()
    for r in range(tok_blocks.shape[0]):
        tok_blocks[r] = tok[:, r * block : (r + 1) * block]

    def prepare():
        own_plan.wait()
        plans = []
        for role in (1, 2, 3):
            pack_copies[role - 1].wait_recv()
            copy = pltpu.make_async_copy(packs.at[role - 1], plan.at[role], plan_sem.at[role])
            copy.start()
            plans.append(copy)
        for copy in plans:
            copy.wait()

    def finish(role):
        for level in range(levels):
            for piece in range(PIECES):
                await_piece(1, role, level, other, piece)

    def migrate():
        for condition, comes, copy in halo_copies:
            when(comes, copy.wait_recv)
        low = h * capacity

        def settle(j, carry):
            source = jnp.int32(cells)
            for d in range(holes + 1):
                slot = low + j - d
                inside = jnp.clip(slot, 0, columns * nonzero - 1)
                c, k = inside // nonzero, lax.rem(inside, nonzero)
                match = jnp.logical_and(slot == inside, plan[0, nonzero + k, c] == low + j)
                source = jnp.where(match, plan[0, k, c], source)
            present = source < cells
            place = source - low
            local = jnp.logical_and(place >= 0, place < capacity)
            inside = jnp.clip(place, 0, capacity - 1)
            beside = jnp.where(place < 0, place + holes, place - capacity + holes)
            beside = jnp.clip(beside, 0, 2 * holes - 1)
            zero = jnp.zeros((block, block), jnp.float32)
            cell = jnp.clip(source, 0, cells - 1)
            for state, moved, index, target in (
                (mas, own, cell, new_mas), (mom, mom_halo, beside, new_mom), (sec, sec_halo, beside, new_sec),
            ):
                value = jnp.where(local, state[inside], moved[index].astype(jnp.float32))
                target[j] = jnp.where(present, value, zero)
            return carry

        lax.fori_loop(0, capacity, settle, 0)

    parts = [columns * i // 4 for i in range(5)]
    order = arrival_order(levels, capacity)
    last = {role: max(i for i, key in enumerate(order) if key[0] == role) for role in range(4)}
    todo = []
    for i, key in enumerate(order):
        handle(*key)
        if todo:
            todo.pop(0)()
        for role in range(3):
            if last[role] == i:
                todo += [send_halo, prepare] if role == 0 else []
                todo += [functools.partial(finish, role)]
                todo += [functools.partial(compute, role, parts[n], parts[n + 1]) for n in range(4)]
    for act in todo:
        act()
    migrate()
    finish(3)

    for condition, copy in sent:
        when(condition, copy.wait_send)
    for copy in pack_copies:
        copy.wait_send()
    for condition, comes, copy in halo_copies:
        when(condition, copy.wait_send)

def on_device_kernel(tokens, master_old, moment_old, second_old, old_cell, new_cell, regrown, new_rows):
    capacity, block = master_old.shape[0], master_old.shape[1]
    columns, nonzero = old_cell.shape
    width, ways = lax.axis_size("dp"), lax.axis_size("fsdp")
    levels, cells, slots = width // 2, width * capacity, columns * nonzero
    holes = cells - slots
    lanes = 128
    listed = jnp.where(regrown == 0, old_cell, cells).T
    pack = jnp.concatenate([listed, new_cell.T], axis=0)
    pack = jnp.pad(pack, ((0, 8 - 2 * nonzero), (0, lanes - columns)))
    token_count = tokens.shape[0]
    bf, f32, i32 = jnp.bfloat16, jnp.float32, jnp.int32
    any_space = pl.BlockSpec(memory_space=pl.ANY)
    vmem, smem = pl.BlockSpec(memory_space=pltpu.VMEM), pl.BlockSpec(memory_space=pltpu.SMEM)
    state = pltpu.VMEM((capacity, block, block), f32)
    narrow = pltpu.VMEM((capacity, block, block), bf)
    halo = pltpu.VMEM((2 * holes, block, block), bf)
    group = pltpu.VMEM((cells + 1, block, block), bf)
    hid = pltpu.VMEM((token_count, columns * block), bf)
    tok_blocks = pltpu.VMEM((tokens.shape[1] // block, token_count, block), bf)
    rows = new_rows.T
    flops = 2 * token_count * slots * block * block
    between = pl.pallas_call(
        functools.partial(kernel, levels, holes, columns, nonzero),
        out_shape=(group, hid, hid, hid, state, state, state, tok_blocks, pltpu.VMEM((3, 8, lanes), i32)),
        in_specs=[vmem, smem, any_space, any_space, any_space, any_space],
        out_specs=(vmem,) * 9,
        scratch_shapes=[
            group, group, group, pltpu.VMEM(tokens.shape, bf), state, state, state, narrow, narrow, halo, halo,
            pltpu.SMEM((4, 8, lanes), i32),
            pltpu.SemaphoreType.DMA((4,)),
            pltpu.SemaphoreType.DMA((4,)),
            pltpu.SemaphoreType.DMA((3,)),
            pltpu.SemaphoreType.DMA((3,)),
            pltpu.SemaphoreType.DMA((2, 2)),
            pltpu.SemaphoreType.DMA((2, 2)),
            pltpu.SemaphoreType.DMA((5, 4, PIECES, levels)),
            pltpu.SemaphoreType.DMA((2, 4, PIECES, levels)),
        ],
        compiler_params=pltpu.CompilerParams(
            collective_id=0, has_side_effects=True, vmem_limit_bytes=KERNEL_VMEM
        ),
        cost_estimate=pl.CostEstimate(
            flops=3 * flops, bytes_accessed=16 * 1024 * 1024, transcendentals=0
        ),
    )(pack, rows, tokens, master_old, moment_old, second_old)
    out_state = jax.ShapeDtypeStruct(master_old.shape, f32)
    return pl.pallas_call(
        functools.partial(last_kernel, columns, nonzero),
        out_shape=(
            jax.ShapeDtypeStruct((token_count, ways * columns * block), bf), out_state, out_state, out_state,
        ),
        in_specs=[vmem] * 9 + [smem],
        out_specs=(any_space,) * 4,
        scratch_shapes=[
            hid,
            pltpu.SMEM((8, lanes), i32),
            pltpu.SemaphoreType.DMA,
            pltpu.SemaphoreType.DMA((10,)),
        ],
        compiler_params=pltpu.CompilerParams(vmem_limit_bytes=LAST_VMEM),
        cost_estimate=pl.CostEstimate(flops=flops, bytes_accessed=8 * 1024 * 1024, transcendentals=0),
    )(*between, rows)


def takes_kernel(mesh, slots, capacity):
    ways, width = mesh.shape["fsdp"], mesh.shape["dp"]
    holes = width * capacity - slots
    return ways == 4 and width % 2 == 0 and PIECES <= capacity and 0 < holes <= capacity and slots <= 512


def solution(mesh):
    def on_device(*args):
        slots, capacity = args[4].size, args[1].shape[0]
        chosen = on_device_kernel if takes_kernel(mesh, slots, capacity) else on_device_plain
        return chosen(*args)

    return jax.shard_map(
        on_device,
        mesh=mesh,
        in_specs=(
            P(("fsdp", "dp"), None),
            P(("fsdp", "dp"), None, None),
            P(("fsdp", "dp"), None, None),
            P(("fsdp", "dp"), None, None),
            P("fsdp", None),
            P("fsdp", None),
            P("fsdp", None),
            P(),
        ),
        out_specs=(
            P(("fsdp", "dp"), None),
            P(("fsdp", "dp"), None, None),
            P(("fsdp", "dp"), None, None),
            P(("fsdp", "dp"), None, None),
        ),
        check_vma=False,
    )
```

```python
import functools

import jax
import jax.numpy as jnp
from jax import lax
from jax.experimental import pallas as pl
from jax.experimental.pallas import tpu as pltpu
from jax.sharding import PartitionSpec as P

MESH = pl.DeviceIdType.MESH
PIECES = 4
X, Y, UP, DOWN, TWIN = range(5)
KERNEL_VMEM = 105 * 1024 * 1024 // 2
LAST_VMEM = 24 * 1024 * 1024


def passed_along(block, axis, distance):
    devices = range(lax.axis_size(axis))
    route = [(i - distance, i) for i in devices if i - distance in devices]
    return lax.ppermute(block, axis, route)


def sources(old_cell, new_cell, regrown, capacity):
    old_flat, new_flat = old_cell.reshape(-1), new_cell.reshape(-1)
    kept = jnp.where(regrown.reshape(-1) == 0, old_flat, -1)
    my_cells = lax.axis_index("dp") * capacity + jnp.arange(capacity, dtype=jnp.int32)
    matches = new_flat[None, :] == my_cells[:, None]
    return jnp.max(jnp.where(matches, kept[None, :], -1), axis=1)


def on_device_plain(tokens, master_old, moment_old, second_old, old_cell, new_cell, regrown, new_rows):
    capacity, block_size = master_old.shape[0], master_old.shape[1]
    column_count, nonzero_count = old_cell.shape
    width = lax.axis_size("dp")
    holes = width * capacity - column_count * nonzero_count
    farthest = min((holes + capacity - 1) // capacity, width - 1)
    holder = lax.axis_index("dp")
    source = sources(old_cell, new_cell, regrown, capacity)
    present = source >= 0
    source = jnp.maximum(source, 0)
    offset = holder - source // capacity
    candidate = jnp.where(offset > 0, 2 * offset - 1, jnp.where(offset < 0, -2 * offset, 0))
    pick_index = candidate * capacity + source % capacity
    shifts = [s for distance in range(1, farthest + 1) for s in (distance, -distance)]

    def settle(state):
        narrow = state.astype(jnp.bfloat16)
        pool = [state] + [passed_along(narrow, "dp", s).astype(jnp.float32) for s in shifts]
        chosen = jnp.take(jnp.concatenate(pool, axis=0), pick_index, axis=0, mode="clip")
        return jnp.where(present[:, None, None], chosen, jnp.float32(0.0))

    cells = lax.all_gather(master_old.astype(jnp.bfloat16), "dp", axis=0, tiled=True)
    panel = jnp.take(cells, old_cell.reshape(-1), axis=0)
    panel = jnp.where(regrown.reshape(-1)[:, None, None] == 0, panel, jnp.bfloat16(0))
    panel = panel.reshape(column_count, nonzero_count, block_size, block_size)
    panel = lax.all_gather(panel, "fsdp", axis=0, tiled=True)
    count, token_count = panel.shape[0], tokens.shape[0]
    token_blocks = tokens.reshape(token_count, tokens.shape[1] // block_size, block_size)
    picked = jnp.take(token_blocks, new_rows.reshape(-1), axis=1)
    picked = picked.reshape(token_count, count, nonzero_count, block_size)
    product = jnp.einsum("tcka,ckab->tcb", picked, panel, preferred_element_type=jnp.float32)
    hidden = product.reshape(token_count, count * block_size).astype(jnp.bfloat16)
    return hidden, settle(master_old), settle(moment_old), settle(second_old)


def onward(levels, z, role, dz, piece):
    steps = []
    if role == 0 or (role == 3 and piece < 2):
        steps += [(DOWN, z - 1, role)] if dz >= 0 and z > 0 else []
        steps += [(UP, z + 1, role)] if dz <= 0 and z < levels - 1 else []
    if role == 0:
        steps += [(X, z, 1), (Y, z, 2)]
    even = (z + dz) % 2 == 0
    if role == 2 and ((piece == 0 and dz == 0) or piece == (2 if even else 3)):
        steps.append((X, z, 3))
    if role == 1 and ((piece == 1 and dz == 0) or piece == (3 if even else 2)):
        steps.append((Y, z, 3))
    return steps


def cuts_of(capacity):
    return [-(-capacity * i // PIECES) for i in range(PIECES + 1)]


def arrival_order(levels, capacity):
    others = [dz for dz in range(1 - levels, levels)]
    cuts = cuts_of(capacity)
    order = [(r, dz, p) for dz in sorted(others, key=abs) for p in range(PIECES) for r in range(4) if r or dz]
    order.sort(key=lambda k: abs(k[1]) + (k[0] in (1, 2)) + 2 * (k[0] == 3))
    best = None
    total = 0.66 * 5.2 * capacity
    for turn in range(14):
        script = [(0, 0, p) for p in range(PIECES)] + order
        arrived, free = {}, {}
        clock, place = [0.0] * levels, [0] * levels
        while True:
            nexts = []
            for z in range(levels):
                while place[z] < len(script) and not 0 <= z + script[place[z]][1] < levels:
                    place[z] += 1
                if place[z] < len(script):
                    role, dz, piece = script[place[z]]
                    came = 0.0 if (role, dz) == (0, 0) else arrived.get((z, role, dz, piece))
                    if came is not None:
                        nexts.append((max(clock[z], came), z))
            if not nexts:
                break
            now, z = min(nexts)
            role, dz, piece = script[place[z]]
            place[z] += 1
            for way, there, role_there in onward(levels, z, role, dz, piece):
                now += 0.15
                free[z, way] = max(free.get((z, way), 0.0), now) + 0.66 * (cuts[piece + 1] - cuts[piece])
                arrived[there, role_there, z + dz - there, piece] = free[z, way] + 1.0
            clock[z] = now + 0.15
        if turn >= 2 and (best is None or max(clock) < best[0]):
            best = (max(clock), order)
        mean = {}
        for key in order:
            came = [arrived[z, key[0], key[1], key[2]] for z in range(levels) if 0 <= z + key[1] < levels]
            held = 0.0
            if key[0] == 3:
                held = 0.87 if key[2] >= 2 else 0.4
            elif key[0] and key[2] >= 2:
                held = 0.68
            mean[key] = max(sum(came) / len(came), held * total)
        order = sorted(order, key=lambda k: (mean[k], k))
    return best[1]


def multiply(tok_blocks, rows_ref, base, group, plan, at, hid, first, last, nonzero):
    block = group.shape[1]
    for c in range(first, last):
        left = [tok_blocks[rows_ref[k, base + c]] for k in range(nonzero)]
        right = [group[plan[(*at, k, c)]] for k in range(nonzero)]
        total = jnp.dot(
            jnp.concatenate(left, axis=1), jnp.concatenate(right, axis=0),
            preferred_element_type=jnp.float32,
        )
        hid[:, c * block : (c + 1) * block] = total.astype(jnp.bfloat16)


def last_kernel(
    columns, nonzero,
    corner, hid0, hid1, hid2, new_mas, new_mom, new_sec, tok_blocks, packs, rows_in,
    hidden_ref, master_out, moment_out, second_out,
    hid3, plan, rows_ref, plan_sem, store_sem,
):
    f = lax.axis_index("fsdp")
    block = corner.shape[1]
    listings = [
        pltpu.make_async_copy(packs.at[2], plan, plan_sem.at[0]),
        pltpu.make_async_copy(rows_in, rows_ref, plan_sem.at[1]),
    ]
    for copy in listings:
        copy.start()
    stores = []

    def store(src, dst):
        copy = pltpu.make_async_copy(src, dst, store_sem.at[len(stores)])
        copy.start()
        stores.append(copy)

    def hidden_part(role, first, last):
        start = pl.multiple_of((jnp.bitwise_xor(f, role) * columns + first) * block, block)
        return hidden_ref.at[:, pl.ds(start, (last - first) * block)]

    for role, hid in enumerate((hid0, hid1, hid2)):
        store(hid, hidden_part(role, 0, columns))
    store(new_mas, master_out)
    store(new_mom, moment_out)
    store(new_sec, second_out)
    for copy in listings:
        copy.wait()
    parts = [columns * i // 4 for i in range(5)]
    for first, last in zip(parts, parts[1:]):
        multiply(tok_blocks, rows_ref, jnp.bitwise_xor(f, 3) * columns, corner, plan, (), hid3, first, last, nonzero)
        store(hid3.at[:, pl.ds(first * block, (last - first) * block)], hidden_part(3, first, last))
    for copy in stores:
        copy.wait()


def kernel(
    levels, holes, columns, nonzero,
    old_in, new_in, regrown_in, rows_in, tokens_ref, master_ref, moment_ref, second_ref,
    corner, hid0, hid1, hid2, new_mas, new_mom, new_sec, tok_blocks, packs,
    own, side_x, side_y, tok, mas, mom, sec, mom_narrow, sec_narrow, mom_halo, sec_halo, plan,
    old_list, new_list, regrown_list, pack_ref, rows_ref, load_sem, plan_sem, pack_send, pack_recv, halo_send, halo_recv, send_sem, recv_sem,
):
    f, h = lax.axis_index("fsdp"), lax.axis_index("dp")
    z, core = h // 2, lax.rem(h, 2)
    capacity, block = mas.shape[0], mas.shape[1]
    cells = 2 * levels * capacity
    cuts = cuts_of(capacity)
    groups = (own, side_x, side_y, corner)
    hids = (hid0, hid1, hid2)

    loads = [
        pltpu.make_async_copy(src, dst, load_sem.at[i])
        for i, (src, dst) in enumerate(
            [
                (master_ref, mas), (moment_ref, mom), (second_ref, sec), (tokens_ref, tok),
                (old_in, old_list), (new_in, new_list), (regrown_in, regrown_list), (rows_in, rows_ref),
            ]
        )
    ]
    for copy in loads:
        copy.start()

    barrier = pltpu.get_barrier_semaphore()

    def at(role, level, which):
        return (jnp.bitwise_xor(f, role), level * 2 + which)

    def greet(device):
        pl.semaphore_signal(barrier, inc=1, device_id=device, device_id_type=MESH)

    up, down = z + 1 < levels, z > 0
    other = 1 - core
    crossing = jnp.where(core == 1, up, down)
    cross_level = jnp.where(core == 1, z + 1, z - 1)

    for group in groups:
        group[cells] = jnp.zeros((block, block), jnp.bfloat16)
    mom_halo[...] = jnp.zeros_like(mom_halo)
    sec_halo[...] = jnp.zeros_like(sec_halo)

    for role in (1, 2, 3):
        greet(at(role, z, core))
    greet(at(0, z, other))

    @pl.when(up)
    def _():
        greet(at(0, z + 1, core))

    @pl.when(down)
    def _():
        greet(at(0, z - 1, core))

    @pl.when(crossing)
    def _():
        greet(at(0, cross_level, other))

    loads[0].wait()
    for j in range(capacity):
        own[h * capacity + j] = mas[j].astype(jnp.bfloat16)
    pl.semaphore_wait(barrier, 4 + up.astype(jnp.int32) + down.astype(jnp.int32) + crossing.astype(jnp.int32))

    sent = []

    def piece_ref(role, level, which, piece):
        first = (level * 2 + which) * capacity + cuts[piece]
        return groups[role].at[pl.ds(first, cuts[piece + 1] - cuts[piece])]

    def when(condition, act):
        if condition is True:
            act()
        else:
            pl.when(condition)(act)

    def send(condition, way, role, level, piece):
        target = {
            X: lambda: at(1, z, core), Y: lambda: at(2, z, core),
            UP: lambda: at(0, z + 1, core), DOWN: lambda: at(0, z - 1, core),
            TWIN: lambda: at(0, z, other),
        }[way]()
        there = role ^ {X: 1, Y: 2}.get(way, 0)
        copy = pltpu.make_async_remote_copy(
            src_ref=piece_ref(role, level, core, piece),
            dst_ref=piece_ref(there, level, core, piece),
            send_sem=send_sem.at[way, role, piece, level],
            recv_sem=recv_sem.at[1 if way == TWIN else 0, there, piece, level],
            device_id=target,
            device_id_type=MESH,
        )
        when(condition, copy.start)
        sent.append((condition, copy))

    def await_piece(lane, role, level, which, piece):
        part = piece_ref(role, level, which, piece)
        pltpu.make_async_remote_copy(
            src_ref=part, dst_ref=part, send_sem=send_sem.at[0, 0, 0, 0],
            recv_sem=recv_sem.at[lane, role, piece, level],
            device_id=at(0, z, other), device_id_type=MESH,
        ).wait_recv()

    def both(a, b):
        if a is True:
            return b
        return jnp.logical_and(a, b)

    def handle(role, dz, piece):
        level = z + dz
        if dz == 0:
            here = True
        else:
            here = level < levels if dz > 0 else level >= 0
        if (role, dz) != (0, 0):
            when(here, lambda: await_piece(0, role, level, core, piece))
        even = lax.rem(level + 2 * levels, 2) == 0
        if role == 0 or (role == 3 and piece < 2):
            if dz >= 0:
                send(both(here, down), DOWN, role, level, piece)
            if dz <= 0:
                send(both(here, up), UP, role, level, piece)
        if role == 0:
            send(here, X, role, level, piece)
            send(here, Y, role, level, piece)
        if role == 2:
            if piece == 0 and dz == 0:
                send(here, X, role, level, piece)
            if piece >= 2:
                send(both(here, even if piece == 2 else jnp.logical_not(even)), X, role, level, piece)
        if role == 1:
            if piece == 1 and dz == 0:
                send(here, Y, role, level, piece)
            if piece >= 2:
                send(both(here, even if piece == 3 else jnp.logical_not(even)), Y, role, level, piece)
        send(here, TWIN, role, level, piece)

    def compute(role, first, last):
        base = jnp.bitwise_xor(f, role) * columns
        multiply(tok_blocks, rows_ref, base, groups[role], plan, (role,), hids[role], first, last, nonzero)

    for piece in range(PIECES):
        handle(0, 0, piece)

    for copy in loads[4:]:
        copy.wait()
    pack_ref[...] = jnp.zeros_like(pack_ref)
    pack_ref[:nonzero, :columns] = jnp.where(regrown_list[...] == 0, old_list[...], cells)
    pack_ref[nonzero : 2 * nonzero, :columns] = new_list[...]
    pack_copies = []
    for role in (1, 2, 3):
        copy = pltpu.make_async_remote_copy(
            src_ref=pack_ref, dst_ref=packs.at[role - 1],
            send_sem=pack_send.at[role - 1], recv_sem=pack_recv.at[role - 1],
            device_id=at(role, z, core), device_id_type=MESH,
        )
        copy.start()
        pack_copies.append(copy)
    own_plan = pltpu.make_async_copy(pack_ref, plan.at[0], plan_sem.at[0])
    own_plan.start()

    halo_copies = []
    right, left = h + 1 < 2 * levels, h > 0
    for i, (narrow, halo) in enumerate(((mom_narrow, mom_halo), (sec_narrow, sec_halo))):
        for side, condition, first, place, holder in (
            (0, right, capacity - holes, 0, h + 1), (1, left, 0, holes, h - 1),
        ):
            copy = pltpu.make_async_remote_copy(
                src_ref=narrow.at[pl.ds(first, holes)], dst_ref=halo.at[pl.ds(place, holes)],
                send_sem=halo_send.at[i, side], recv_sem=halo_recv.at[i, side],
                device_id=(f, holder), device_id_type=MESH,
            )
            halo_copies.append((condition, left if side == 0 else right, copy))

    def send_halo():
        for condition, comes, copy in halo_copies:
            when(condition, copy.start)

    loads[1].wait()
    loads[2].wait()
    for state, narrow in ((mom, mom_narrow), (sec, sec_narrow)):
        for j in range(capacity):
            narrow[j] = state[j].astype(jnp.bfloat16)
    loads[3].wait()
    for r in range(tok_blocks.shape[0]):
        tok_blocks[r] = tok[:, r * block : (r + 1) * block]

    def prepare():
        own_plan.wait()
        plans = []
        for role in (1, 2, 3):
            pack_copies[role - 1].wait_recv()
            copy = pltpu.make_async_copy(packs.at[role - 1], plan.at[role], plan_sem.at[role])
            copy.start()
            plans.append(copy)
        for copy in plans:
            copy.wait()

    def finish(role):
        for level in range(levels):
            for piece in range(PIECES):
                await_piece(1, role, level, other, piece)

    def migrate():
        for condition, comes, copy in halo_copies:
            when(comes, copy.wait_recv)
        low = h * capacity

        def settle(j, carry):
            source = jnp.int32(cells)
            for d in range(holes + 1):
                slot = low + j - d
                inside = jnp.clip(slot, 0, columns * nonzero - 1)
                c, k = inside // nonzero, lax.rem(inside, nonzero)
                match = jnp.logical_and(slot == inside, plan[0, nonzero + k, c] == low + j)
                source = jnp.where(match, plan[0, k, c], source)
            present = source < cells
            place = source - low
            local = jnp.logical_and(place >= 0, place < capacity)
            inside = jnp.clip(place, 0, capacity - 1)
            beside = jnp.where(place < 0, place + holes, place - capacity + holes)
            beside = jnp.clip(beside, 0, 2 * holes - 1)
            zero = jnp.zeros((block, block), jnp.float32)
            cell = jnp.clip(source, 0, cells - 1)
            for state, moved, index, target in (
                (mas, own, cell, new_mas), (mom, mom_halo, beside, new_mom), (sec, sec_halo, beside, new_sec),
            ):
                value = jnp.where(local, state[inside], moved[index].astype(jnp.float32))
                target[j] = jnp.where(present, value, zero)
            return carry

        lax.fori_loop(0, capacity, settle, 0)

    parts = [columns * i // 4 for i in range(5)]
    order = arrival_order(levels, capacity)
    last = {role: max(i for i, key in enumerate(order) if key[0] == role) for role in range(4)}
    todo = []
    for i, key in enumerate(order):
        handle(*key)
        if todo:
            todo.pop(0)()
        for role in range(3):
            if last[role] == i:
                todo += [send_halo, prepare] if role == 0 else []
                todo += [functools.partial(finish, role)]
                todo += [functools.partial(compute, role, parts[n], parts[n + 1]) for n in range(4)]
    for act in todo:
        act()
    migrate()
    finish(3)

    for condition, copy in sent:
        when(condition, copy.wait_send)
    for copy in pack_copies:
        copy.wait_send()
    for condition, comes, copy in halo_copies:
        when(condition, copy.wait_send)

def on_device_kernel(tokens, master_old, moment_old, second_old, old_cell, new_cell, regrown, new_rows):
    capacity, block = master_old.shape[0], master_old.shape[1]
    columns, nonzero = old_cell.shape
    width, ways = lax.axis_size("dp"), lax.axis_size("fsdp")
    levels, cells, slots = width // 2, width * capacity, columns * nonzero
    holes = cells - slots
    lanes = 128
    token_count = tokens.shape[0]
    bf, f32, i32 = jnp.bfloat16, jnp.float32, jnp.int32
    any_space = pl.BlockSpec(memory_space=pl.ANY)
    vmem = pl.BlockSpec(memory_space=pltpu.VMEM)
    state = pltpu.VMEM((capacity, block, block), f32)
    narrow = pltpu.VMEM((capacity, block, block), bf)
    halo = pltpu.VMEM((2 * holes, block, block), bf)
    group = pltpu.VMEM((cells + 1, block, block), bf)
    hid = pltpu.VMEM((token_count, columns * block), bf)
    tok_blocks = pltpu.VMEM((tokens.shape[1] // block, token_count, block), bf)
    rows = new_rows.T
    listed = pltpu.VMEM((nonzero, columns), i32)
    flops = 2 * token_count * slots * block * block
    between = pl.pallas_call(
        functools.partial(kernel, levels, holes, columns, nonzero),
        out_shape=(group, hid, hid, hid, state, state, state, tok_blocks, pltpu.VMEM((3, 8, lanes), i32)),
        in_specs=[any_space] * 8,
        out_specs=(vmem,) * 9,
        scratch_shapes=[
            group, group, group, pltpu.VMEM(tokens.shape, bf), state, state, state, narrow, narrow, halo, halo,
            pltpu.SMEM((4, 8, lanes), i32),
            listed, listed, listed, pltpu.VMEM((8, lanes), i32), pltpu.SMEM(rows.shape, i32),
            pltpu.SemaphoreType.DMA((8,)),
            pltpu.SemaphoreType.DMA((4,)),
            pltpu.SemaphoreType.DMA((3,)),
            pltpu.SemaphoreType.DMA((3,)),
            pltpu.SemaphoreType.DMA((2, 2)),
            pltpu.SemaphoreType.DMA((2, 2)),
            pltpu.SemaphoreType.DMA((5, 4, PIECES, levels)),
            pltpu.SemaphoreType.DMA((2, 4, PIECES, levels)),
        ],
        compiler_params=pltpu.CompilerParams(
            collective_id=0, has_side_effects=True, vmem_limit_bytes=KERNEL_VMEM
        ),
        cost_estimate=pl.CostEstimate(
            flops=3 * flops, bytes_accessed=16 * 1024 * 1024, transcendentals=0
        ),
    )(old_cell.T, new_cell.T, regrown.T, rows, tokens, master_old, moment_old, second_old)
    out_state = jax.ShapeDtypeStruct(master_old.shape, f32)
    return pl.pallas_call(
        functools.partial(last_kernel, columns, nonzero),
        out_shape=(
            jax.ShapeDtypeStruct((token_count, ways * columns * block), bf), out_state, out_state, out_state,
        ),
        in_specs=[vmem] * 9 + [any_space],
        out_specs=(any_space,) * 4,
        scratch_shapes=[
            hid,
            pltpu.SMEM((8, lanes), i32),
            pltpu.SMEM(rows.shape, i32),
            pltpu.SemaphoreType.DMA((2,)),
            pltpu.SemaphoreType.DMA((10,)),
        ],
        compiler_params=pltpu.CompilerParams(vmem_limit_bytes=LAST_VMEM),
        cost_estimate=pl.CostEstimate(flops=flops, bytes_accessed=8 * 1024 * 1024, transcendentals=0),
    )(*between, rows)


def takes_kernel(mesh, slots, capacity):
    ways, width = mesh.shape["fsdp"], mesh.shape["dp"]
    holes = width * capacity - slots
    return ways == 4 and width % 2 == 0 and PIECES <= capacity and 0 < holes <= capacity and slots <= 512


def solution(mesh):
    def on_device(*args):
        slots, capacity = args[4].size, args[1].shape[0]
        chosen = on_device_kernel if takes_kernel(mesh, slots, capacity) else on_device_plain
        return chosen(*args)

    return jax.shard_map(
        on_device,
        mesh=mesh,
        in_specs=(
            P(("fsdp", "dp"), None),
            P(("fsdp", "dp"), None, None),
            P(("fsdp", "dp"), None, None),
            P(("fsdp", "dp"), None, None),
            P("fsdp", None),
            P("fsdp", None),
            P("fsdp", None),
            P(),
        ),
        out_specs=(
            P(("fsdp", "dp"), None),
            P(("fsdp", "dp"), None, None),
            P(("fsdp", "dp"), None, None),
            P(("fsdp", "dp"), None, None),
        ),
        check_vma=False,
    )
```

```python
import functools

import jax
import jax.numpy as jnp
from jax import lax
from jax.experimental import pallas as pl
from jax.experimental.pallas import tpu as pltpu
from jax.sharding import PartitionSpec as P

MESH = pl.DeviceIdType.MESH
PIECES = 4
X, Y, UP, DOWN, TWIN = range(5)
KERNEL_VMEM = 105 * 1024 * 1024 // 2
LAST_VMEM = 24 * 1024 * 1024


def passed_along(block, axis, distance):
    devices = range(lax.axis_size(axis))
    route = [(i - distance, i) for i in devices if i - distance in devices]
    return lax.ppermute(block, axis, route)


def sources(old_cell, new_cell, regrown, capacity):
    old_flat, new_flat = old_cell.reshape(-1), new_cell.reshape(-1)
    kept = jnp.where(regrown.reshape(-1) == 0, old_flat, -1)
    my_cells = lax.axis_index("dp") * capacity + jnp.arange(capacity, dtype=jnp.int32)
    matches = new_flat[None, :] == my_cells[:, None]
    return jnp.max(jnp.where(matches, kept[None, :], -1), axis=1)


def on_device_plain(tokens, master_old, moment_old, second_old, old_cell, new_cell, regrown, new_rows):
    capacity, block_size = master_old.shape[0], master_old.shape[1]
    column_count, nonzero_count = old_cell.shape
    width = lax.axis_size("dp")
    holes = width * capacity - column_count * nonzero_count
    farthest = min((holes + capacity - 1) // capacity, width - 1)
    holder = lax.axis_index("dp")
    source = sources(old_cell, new_cell, regrown, capacity)
    present = source >= 0
    source = jnp.maximum(source, 0)
    offset = holder - source // capacity
    candidate = jnp.where(offset > 0, 2 * offset - 1, jnp.where(offset < 0, -2 * offset, 0))
    pick_index = candidate * capacity + source % capacity
    shifts = [s for distance in range(1, farthest + 1) for s in (distance, -distance)]

    def settle(state):
        narrow = state.astype(jnp.bfloat16)
        pool = [state] + [passed_along(narrow, "dp", s).astype(jnp.float32) for s in shifts]
        chosen = jnp.take(jnp.concatenate(pool, axis=0), pick_index, axis=0, mode="clip")
        return jnp.where(present[:, None, None], chosen, jnp.float32(0.0))

    cells = lax.all_gather(master_old.astype(jnp.bfloat16), "dp", axis=0, tiled=True)
    panel = jnp.take(cells, old_cell.reshape(-1), axis=0)
    panel = jnp.where(regrown.reshape(-1)[:, None, None] == 0, panel, jnp.bfloat16(0))
    panel = panel.reshape(column_count, nonzero_count, block_size, block_size)
    panel = lax.all_gather(panel, "fsdp", axis=0, tiled=True)
    count, token_count = panel.shape[0], tokens.shape[0]
    token_blocks = tokens.reshape(token_count, tokens.shape[1] // block_size, block_size)
    picked = jnp.take(token_blocks, new_rows.reshape(-1), axis=1)
    picked = picked.reshape(token_count, count, nonzero_count, block_size)
    product = jnp.einsum("tcka,ckab->tcb", picked, panel, preferred_element_type=jnp.float32)
    hidden = product.reshape(token_count, count * block_size).astype(jnp.bfloat16)
    return hidden, settle(master_old), settle(moment_old), settle(second_old)


def onward(levels, z, role, dz, piece):
    steps = []
    if role == 0 or (role == 3 and piece < 2):
        steps += [(DOWN, z - 1, role)] if dz >= 0 and z > 0 else []
        steps += [(UP, z + 1, role)] if dz <= 0 and z < levels - 1 else []
    if role == 0:
        steps += [(X, z, 1), (Y, z, 2)]
    even = (z + dz) % 2 == 0
    if role == 2 and ((piece == 0 and dz == 0) or piece == (2 if even else 3)):
        steps.append((X, z, 3))
    if role == 1 and ((piece == 1 and dz == 0) or piece == (3 if even else 2)):
        steps.append((Y, z, 3))
    return steps


def cuts_of(capacity):
    return [-(-capacity * i // PIECES) for i in range(PIECES + 1)]


def arrival_order(levels, capacity):
    others = [dz for dz in range(1 - levels, levels)]
    cuts = cuts_of(capacity)
    order = [(r, dz, p) for dz in sorted(others, key=abs) for p in range(PIECES) for r in range(4) if r or dz]
    order.sort(key=lambda k: abs(k[1]) + (k[0] in (1, 2)) + 2 * (k[0] == 3))
    best = None
    total = 0.74 * 5.2 * capacity
    for turn in range(14):
        script = [(0, 0, p) for p in range(PIECES)] + order
        arrived, free = {}, {}
        clock, place = [0.0] * levels, [0] * levels
        while True:
            nexts = []
            for z in range(levels):
                while place[z] < len(script) and not 0 <= z + script[place[z]][1] < levels:
                    place[z] += 1
                if place[z] < len(script):
                    role, dz, piece = script[place[z]]
                    came = 0.0 if (role, dz) == (0, 0) else arrived.get((z, role, dz, piece))
                    if came is not None:
                        nexts.append((max(clock[z], came), z))
            if not nexts:
                break
            now, z = min(nexts)
            role, dz, piece = script[place[z]]
            place[z] += 1
            for way, there, role_there in onward(levels, z, role, dz, piece):
                now += 0.15
                free[z, way] = max(free.get((z, way), 0.0), now) + 0.74 * (cuts[piece + 1] - cuts[piece])
                arrived[there, role_there, z + dz - there, piece] = free[z, way] + 1.0
            clock[z] = now + 0.15
        if turn >= 2 and (best is None or max(clock) < best[0]):
            best = (max(clock), order)
        mean = {}
        for key in order:
            came = [arrived[z, key[0], key[1], key[2]] for z in range(levels) if 0 <= z + key[1] < levels]
            held = 0.0
            if key[0] == 3:
                held = 0.87 if key[2] >= 2 else 0.55
            elif key[0] and key[2] >= 2:
                held = 0.6
            mean[key] = max(sum(came) / len(came), held * total)
        order = sorted(order, key=lambda k: (mean[k], k))
    return best[1]


def multiply(tok_blocks, rows_ref, base, group, plan, at, hid, first, last, nonzero):
    block = group.shape[1]
    for c in range(first, last):
        left = [tok_blocks[rows_ref[k, base + c]] for k in range(nonzero)]
        right = [group[plan[(*at, k, c)]] for k in range(nonzero)]
        total = jnp.dot(
            jnp.concatenate(left, axis=1), jnp.concatenate(right, axis=0),
            preferred_element_type=jnp.float32,
        )
        hid[:, c * block : (c + 1) * block] = total.astype(jnp.bfloat16)


def last_kernel(
    columns, nonzero,
    corner, hid0, hid1, hid2, new_mas, new_mom, new_sec, tok_blocks, packs, rows_in,
    hidden_ref, master_out, moment_out, second_out,
    hid3, plan, rows_ref, plan_sem, store_sem,
):
    f = lax.axis_index("fsdp")
    block = corner.shape[1]
    listings = [
        pltpu.make_async_copy(packs.at[2], plan, plan_sem.at[0]),
        pltpu.make_async_copy(rows_in, rows_ref, plan_sem.at[1]),
    ]
    for copy in listings:
        copy.start()
    stores = []

    def store(src, dst):
        copy = pltpu.make_async_copy(src, dst, store_sem.at[len(stores)])
        copy.start()
        stores.append(copy)

    def hidden_part(role, first, last):
        start = pl.multiple_of((jnp.bitwise_xor(f, role) * columns + first) * block, block)
        return hidden_ref.at[:, pl.ds(start, (last - first) * block)]

    for role, hid in enumerate((hid0, hid1, hid2)):
        store(hid, hidden_part(role, 0, columns))
    store(new_mas, master_out)
    store(new_mom, moment_out)
    store(new_sec, second_out)
    for copy in listings:
        copy.wait()
    parts = [columns * i // 4 for i in range(5)]
    for first, last in zip(parts, parts[1:]):
        multiply(tok_blocks, rows_ref, jnp.bitwise_xor(f, 3) * columns, corner, plan, (), hid3, first, last, nonzero)
        store(hid3.at[:, pl.ds(first * block, (last - first) * block)], hidden_part(3, first, last))
    for copy in stores:
        copy.wait()


def kernel(
    levels, holes, columns, nonzero,
    old_in, new_in, regrown_in, rows_in, tokens_ref, master_ref, moment_ref, second_ref,
    corner, hid0, hid1, hid2, new_mas, new_mom, new_sec, tok_blocks, packs,
    own, side_x, side_y, tok, mas, mom, sec, mom_narrow, sec_narrow, mom_halo, sec_halo, plan,
    old_list, new_list, regrown_list, pack_ref, rows_ref, load_sem, plan_sem, pack_send, pack_recv, halo_send, halo_recv, send_sem, recv_sem,
):
    f, h = lax.axis_index("fsdp"), lax.axis_index("dp")
    z, core = h // 2, lax.rem(h, 2)
    capacity, block = mas.shape[0], mas.shape[1]
    cells = 2 * levels * capacity
    cuts = cuts_of(capacity)
    groups = (own, side_x, side_y, corner)
    hids = (hid0, hid1, hid2)

    loads = [
        pltpu.make_async_copy(src, dst, load_sem.at[i])
        for i, (src, dst) in enumerate(
            [
                (master_ref, mas), (moment_ref, mom), (second_ref, sec), (tokens_ref, tok),
                (old_in, old_list), (new_in, new_list), (regrown_in, regrown_list), (rows_in, rows_ref),
            ]
        )
    ]
    for copy in loads:
        copy.start()

    barrier = pltpu.get_barrier_semaphore()

    def at(role, level, which):
        return (jnp.bitwise_xor(f, role), level * 2 + which)

    def greet(device):
        pl.semaphore_signal(barrier, inc=1, device_id=device, device_id_type=MESH)

    up, down = z + 1 < levels, z > 0
    other = 1 - core
    crossing = jnp.where(core == 1, up, down)
    cross_level = jnp.where(core == 1, z + 1, z - 1)

    for group in groups:
        group[cells] = jnp.zeros((block, block), jnp.bfloat16)
    mom_halo[...] = jnp.zeros_like(mom_halo)
    sec_halo[...] = jnp.zeros_like(sec_halo)

    for role in (1, 2, 3):
        greet(at(role, z, core))
    greet(at(0, z, other))

    @pl.when(up)
    def _():
        greet(at(0, z + 1, core))

    @pl.when(down)
    def _():
        greet(at(0, z - 1, core))

    @pl.when(crossing)
    def _():
        greet(at(0, cross_level, other))

    loads[0].wait()
    for j in range(capacity):
        own[h * capacity + j] = mas[j].astype(jnp.bfloat16)
    pl.semaphore_wait(barrier, 4 + up.astype(jnp.int32) + down.astype(jnp.int32) + crossing.astype(jnp.int32))

    sent = []

    def piece_ref(role, level, which, piece):
        first = (level * 2 + which) * capacity + cuts[piece]
        return groups[role].at[pl.ds(first, cuts[piece + 1] - cuts[piece])]

    def when(condition, act):
        if condition is True:
            act()
        else:
            pl.when(condition)(act)

    def send(condition, way, role, level, piece):
        target = {
            X: lambda: at(1, z, core), Y: lambda: at(2, z, core),
            UP: lambda: at(0, z + 1, core), DOWN: lambda: at(0, z - 1, core),
            TWIN: lambda: at(0, z, other),
        }[way]()
        there = role ^ {X: 1, Y: 2}.get(way, 0)
        copy = pltpu.make_async_remote_copy(
            src_ref=piece_ref(role, level, core, piece),
            dst_ref=piece_ref(there, level, core, piece),
            send_sem=send_sem.at[way, role, piece, level],
            recv_sem=recv_sem.at[1 if way == TWIN else 0, there, piece, level],
            device_id=target,
            device_id_type=MESH,
        )
        when(condition, copy.start)
        sent.append((condition, copy))

    def await_piece(lane, role, level, which, piece):
        part = piece_ref(role, level, which, piece)
        pltpu.make_async_remote_copy(
            src_ref=part, dst_ref=part, send_sem=send_sem.at[0, 0, 0, 0],
            recv_sem=recv_sem.at[lane, role, piece, level],
            device_id=at(0, z, other), device_id_type=MESH,
        ).wait_recv()

    def both(a, b):
        if a is True:
            return b
        return jnp.logical_and(a, b)

    def handle(role, dz, piece):
        level = z + dz
        if dz == 0:
            here = True
        else:
            here = level < levels if dz > 0 else level >= 0
        if (role, dz) != (0, 0):
            when(here, lambda: await_piece(0, role, level, core, piece))
        even = lax.rem(level + 2 * levels, 2) == 0
        if role == 0 or (role == 3 and piece < 2):
            if dz >= 0:
                send(both(here, down), DOWN, role, level, piece)
            if dz <= 0:
                send(both(here, up), UP, role, level, piece)
        if role == 0:
            send(here, X, role, level, piece)
            send(here, Y, role, level, piece)
        if role == 2:
            if piece == 0 and dz == 0:
                send(here, X, role, level, piece)
            if piece >= 2:
                send(both(here, even if piece == 2 else jnp.logical_not(even)), X, role, level, piece)
        if role == 1:
            if piece == 1 and dz == 0:
                send(here, Y, role, level, piece)
            if piece >= 2:
                send(both(here, even if piece == 3 else jnp.logical_not(even)), Y, role, level, piece)
        send(here, TWIN, role, level, piece)

    def compute(role, first, last):
        base = jnp.bitwise_xor(f, role) * columns
        multiply(tok_blocks, rows_ref, base, groups[role], plan, (role,), hids[role], first, last, nonzero)

    for piece in range(PIECES):
        handle(0, 0, piece)

    for copy in loads[4:]:
        copy.wait()
    pack_ref[...] = jnp.zeros_like(pack_ref)
    pack_ref[:nonzero, :columns] = jnp.where(regrown_list[...] == 0, old_list[...], cells)
    pack_ref[nonzero : 2 * nonzero, :columns] = new_list[...]
    pack_copies = []
    for role in (1, 2, 3):
        copy = pltpu.make_async_remote_copy(
            src_ref=pack_ref, dst_ref=packs.at[role - 1],
            send_sem=pack_send.at[role - 1], recv_sem=pack_recv.at[role - 1],
            device_id=at(role, z, core), device_id_type=MESH,
        )
        copy.start()
        pack_copies.append(copy)
    own_plan = pltpu.make_async_copy(pack_ref, plan.at[0], plan_sem.at[0])
    own_plan.start()

    halo_copies = []
    right, left = h + 1 < 2 * levels, h > 0
    for i, (narrow, halo) in enumerate(((mom_narrow, mom_halo), (sec_narrow, sec_halo))):
        for side, condition, first, place, holder in (
            (0, right, capacity - holes, 0, h + 1), (1, left, 0, holes, h - 1),
        ):
            copy = pltpu.make_async_remote_copy(
                src_ref=narrow.at[pl.ds(first, holes)], dst_ref=halo.at[pl.ds(place, holes)],
                send_sem=halo_send.at[i, side], recv_sem=halo_recv.at[i, side],
                device_id=(f, holder), device_id_type=MESH,
            )
            halo_copies.append((condition, left if side == 0 else right, copy))

    def send_halo():
        for condition, comes, copy in halo_copies:
            when(condition, copy.start)

    loads[1].wait()
    loads[2].wait()
    for state, narrow in ((mom, mom_narrow), (sec, sec_narrow)):
        for j in range(capacity):
            narrow[j] = state[j].astype(jnp.bfloat16)
    loads[3].wait()
    for r in range(tok_blocks.shape[0]):
        tok_blocks[r] = tok[:, r * block : (r + 1) * block]

    def prepare():
        own_plan.wait()
        plans = []
        for role in (1, 2, 3):
            pack_copies[role - 1].wait_recv()
            copy = pltpu.make_async_copy(packs.at[role - 1], plan.at[role], plan_sem.at[role])
            copy.start()
            plans.append(copy)
        for copy in plans:
            copy.wait()

    def finish(role):
        for level in range(levels):
            for piece in range(PIECES):
                await_piece(1, role, level, other, piece)

    def migrate():
        for condition, comes, copy in halo_copies:
            when(comes, copy.wait_recv)
        low = h * capacity

        def settle(j, carry):
            source = jnp.int32(cells)
            for d in range(holes + 1):
                slot = low + j - d
                inside = jnp.clip(slot, 0, columns * nonzero - 1)
                c, k = inside // nonzero, lax.rem(inside, nonzero)
                match = jnp.logical_and(slot == inside, plan[0, nonzero + k, c] == low + j)
                source = jnp.where(match, plan[0, k, c], source)
            present = source < cells
            place = source - low
            local = jnp.logical_and(place >= 0, place < capacity)
            inside = jnp.clip(place, 0, capacity - 1)
            beside = jnp.where(place < 0, place + holes, place - capacity + holes)
            beside = jnp.clip(beside, 0, 2 * holes - 1)
            zero = jnp.zeros((block, block), jnp.float32)
            cell = jnp.clip(source, 0, cells - 1)
            for state, moved, index, target in (
                (mas, own, cell, new_mas), (mom, mom_halo, beside, new_mom), (sec, sec_halo, beside, new_sec),
            ):
                value = jnp.where(local, state[inside], moved[index].astype(jnp.float32))
                target[j] = jnp.where(present, value, zero)
            return carry

        lax.fori_loop(0, capacity, settle, 0)

    parts = [columns * i // 4 for i in range(5)]
    order = arrival_order(levels, capacity)
    last = {role: max(i for i, key in enumerate(order) if key[0] == role) for role in range(4)}
    todo = []
    for i, key in enumerate(order):
        handle(*key)
        if todo:
            todo.pop(0)()
        for role in range(3):
            if last[role] == i:
                todo += [send_halo, prepare] if role == 0 else []
                todo += [functools.partial(finish, role)]
                todo += [functools.partial(compute, role, parts[n], parts[n + 1]) for n in range(4)]
                todo += [migrate] if last[role] == max(last[r] for r in range(3)) else []
    for act in todo:
        act()
    finish(3)

    for condition, copy in sent:
        when(condition, copy.wait_send)
    for copy in pack_copies:
        copy.wait_send()
    for condition, comes, copy in halo_copies:
        when(condition, copy.wait_send)

def on_device_kernel(tokens, master_old, moment_old, second_old, old_cell, new_cell, regrown, new_rows):
    capacity, block = master_old.shape[0], master_old.shape[1]
    columns, nonzero = old_cell.shape
    width, ways = lax.axis_size("dp"), lax.axis_size("fsdp")
    levels, cells, slots = width // 2, width * capacity, columns * nonzero
    holes = cells - slots
    lanes = 128
    token_count = tokens.shape[0]
    bf, f32, i32 = jnp.bfloat16, jnp.float32, jnp.int32
    any_space = pl.BlockSpec(memory_space=pl.ANY)
    vmem = pl.BlockSpec(memory_space=pltpu.VMEM)
    state = pltpu.VMEM((capacity, block, block), f32)
    narrow = pltpu.VMEM((capacity, block, block), bf)
    halo = pltpu.VMEM((2 * holes, block, block), bf)
    group = pltpu.VMEM((cells + 1, block, block), bf)
    hid = pltpu.VMEM((token_count, columns * block), bf)
    tok_blocks = pltpu.VMEM((tokens.shape[1] // block, token_count, block), bf)
    rows = new_rows.T
    listed = pltpu.VMEM((nonzero, columns), i32)
    flops = 2 * token_count * slots * block * block
    between = pl.pallas_call(
        functools.partial(kernel, levels, holes, columns, nonzero),
        out_shape=(group, hid, hid, hid, state, state, state, tok_blocks, pltpu.VMEM((3, 8, lanes), i32)),
        in_specs=[any_space] * 8,
        out_specs=(vmem,) * 9,
        scratch_shapes=[
            group, group, group, pltpu.VMEM(tokens.shape, bf), state, state, state, narrow, narrow, halo, halo,
            pltpu.SMEM((4, 8, lanes), i32),
            listed, listed, listed, pltpu.VMEM((8, lanes), i32), pltpu.SMEM(rows.shape, i32),
            pltpu.SemaphoreType.DMA((8,)),
            pltpu.SemaphoreType.DMA((4,)),
            pltpu.SemaphoreType.DMA((3,)),
            pltpu.SemaphoreType.DMA((3,)),
            pltpu.SemaphoreType.DMA((2, 2)),
            pltpu.SemaphoreType.DMA((2, 2)),
            pltpu.SemaphoreType.DMA((5, 4, PIECES, levels)),
            pltpu.SemaphoreType.DMA((2, 4, PIECES, levels)),
        ],
        compiler_params=pltpu.CompilerParams(
            collective_id=0, has_side_effects=True, vmem_limit_bytes=KERNEL_VMEM
        ),
        cost_estimate=pl.CostEstimate(
            flops=3 * flops, bytes_accessed=16 * 1024 * 1024, transcendentals=0
        ),
    )(old_cell.T, new_cell.T, regrown.T, rows, tokens, master_old, moment_old, second_old)
    out_state = jax.ShapeDtypeStruct(master_old.shape, f32)
    return pl.pallas_call(
        functools.partial(last_kernel, columns, nonzero),
        out_shape=(
            jax.ShapeDtypeStruct((token_count, ways * columns * block), bf), out_state, out_state, out_state,
        ),
        in_specs=[vmem] * 9 + [any_space],
        out_specs=(any_space,) * 4,
        scratch_shapes=[
            hid,
            pltpu.SMEM((8, lanes), i32),
            pltpu.SMEM(rows.shape, i32),
            pltpu.SemaphoreType.DMA((2,)),
            pltpu.SemaphoreType.DMA((10,)),
        ],
        compiler_params=pltpu.CompilerParams(vmem_limit_bytes=LAST_VMEM),
        cost_estimate=pl.CostEstimate(flops=flops, bytes_accessed=8 * 1024 * 1024, transcendentals=0),
    )(*between, rows)


def takes_kernel(mesh, slots, capacity):
    ways, width = mesh.shape["fsdp"], mesh.shape["dp"]
    holes = width * capacity - slots
    return ways == 4 and width % 2 == 0 and PIECES <= capacity and 0 < holes <= capacity and slots <= 512


def solution(mesh):
    def on_device(*args):
        slots, capacity = args[4].size, args[1].shape[0]
        chosen = on_device_kernel if takes_kernel(mesh, slots, capacity) else on_device_plain
        return chosen(*args)

    return jax.shard_map(
        on_device,
        mesh=mesh,
        in_specs=(
            P(("fsdp", "dp"), None),
            P(("fsdp", "dp"), None, None),
            P(("fsdp", "dp"), None, None),
            P(("fsdp", "dp"), None, None),
            P("fsdp", None),
            P("fsdp", None),
            P("fsdp", None),
            P(),
        ),
        out_specs=(
            P(("fsdp", "dp"), None),
            P(("fsdp", "dp"), None, None),
            P(("fsdp", "dp"), None, None),
            P(("fsdp", "dp"), None, None),
        ),
        check_vma=False,
    )
```
